32 devices in a mesh: harm: 4 (over z), node: 8 (over y, x, core).
Axes of the slice: x: 2, y: 2, z: 4, core: 2. Of those that a mesh axis runs over, the one named last changes fastest.
Arguments:
- adjoint: bfloat16 [128, 4, 32768], P('harm', None, 'node'), may hold values from -6 to 6
- source: float32 [128, 131072], P(None, ('harm', 'node')), may hold values from -6 to 6
- rad_coeff: bfloat16 [128, 131072], P(None, ('harm', 'node')), may hold values from 0.19921875 to 2
- capacity: float32 [131072], P(('harm', 'node')), may hold values from 0.005 to 0.03
- inv_diag: float32 [131072], P(('harm', 'node')), may hold values from 0.1 to 0.5
- blocks: bfloat16 [1024, 4, 128, 128], P(('harm', 'node')), may hold values from -0.25 to 0.25
- block_cols: int32 [1024, 4], P(('harm', 'node')), may hold values from 0 to 1023, as said below
- zone_of: int32 [131072], P(('harm', 'node')), may hold values from 0 to 1279, as said below
- heater_weight: float32 [131072], P(('harm', 'node')), may hold values from 0.2 to 2
Outputs:
- updated: bfloat16 [128, 4, 32768], P('harm', None, 'node')
- gradient: float32 [1280, 128], P(('harm', 'node'))
The draws below stay inside these ranges and needn't reach their ends.
Inputs may be any that keep to these rules, and one draw needn't show every extreme that they name: `block_cols`: with d = b // 32 and D = 32: slot 0 of row block b names b itself; slot 1 lies in row blocks max(d - 1, 0) * 32 to (max(d - 1, 0) + 1) * 32 - 1; slot 2 in min(d + 1, D - 1) * 32 to (min(d + 1, D - 1) + 1) * 32 - 1; the other slots in (d - 1) * 32 to (d + 2) * 32 - 1. `zone_of`: node n lies in a zone z with (n // 4096 - 1) * 40 <= z < (n // 4096 + 2) * 40.
All inputs are finite; a program needn't handle non-finite values.
Results may differ from the reference program's by a relative error of at most 0.0035.
Values may be sent and summed in bfloat16 or wider, within the bound.
A program may use at most 64 MiB of HBM per device.

```python
import math
import jax
import jax.numpy as jnp
from jax import lax

K = 128
P_SIZE = 128
BLK = 128
NNZ = 4
SUB = 4096
ZONE_DEV = 40
NODES = 131072
NBLK = 1024
RB = 32
ZONES = 1280
N_HARM = 4
N_NODE = 8


def draw_block_cols(key, part):
    key_low = jax.random.fold_in(key, 21)
    key_high = jax.random.fold_in(key, 22)
    key_rest = jax.random.fold_in(key, 23)
    row_device = jnp.arange(NBLK, dtype=jnp.int32) // RB
    device_total = NBLK // RB
    lower = jnp.maximum(row_device - 1, 0) * RB
    upper = jnp.minimum(row_device + 2, device_total) * RB
    low_dev = jnp.maximum(row_device - 1, 0)
    high_dev = jnp.minimum(row_device + 1, device_total - 1)
    low_pick = low_dev * RB + jax.random.randint(key_low, (NBLK,), 0, RB, dtype=jnp.int32)
    high_pick = high_dev * RB + jax.random.randint(key_high, (NBLK,), 0, RB, dtype=jnp.int32)
    picked = jax.random.randint(key_rest, (NBLK, NNZ), lower[:, None], upper[:, None], dtype=jnp.int32)
    picked = picked.at[:, 0].set(jnp.arange(NBLK, dtype=jnp.int32))
    picked = picked.at[:, 1].set(low_pick)
    picked = picked.at[:, 2].set(high_pick)
    return picked.astype(jnp.int32)


def draw_zone_of(key, part):
    key_spill = jax.random.fold_in(key, 11)
    key_side = jax.random.fold_in(key, 12)
    key_pick = jax.random.fold_in(key, 13)
    node_index = jnp.arange(NODES, dtype=jnp.int32)
    device_total = NODES // SUB
    owner = node_index // SUB
    inside = node_index % SUB
    home_zone = owner * ZONE_DEV + inside * ZONE_DEV // SUB
    spilled = jax.random.randint(key_spill, (NODES,), 0, 4, dtype=jnp.int32) == 0
    side_step = jax.random.randint(key_side, (NODES,), 0, 2, dtype=jnp.int32) * 2 - 1
    target = owner + side_step
    usable = (target >= 0) & (target < device_total)
    other_zone = target * ZONE_DEV + jax.random.randint(key_pick, (NODES,), 0, ZONE_DEV, dtype=jnp.int32)
    return jnp.where(spilled & usable, other_zone, home_zone).astype(jnp.int32)


def shard_levels(stream_key, shape, cuts, low, high):
    loudness = 1.0
    for position, shards_of in cuts:
        steps = jax.random.uniform(jax.random.fold_in(jax.random.fold_in(stream_key, 6), position), (shards_of,), jnp.float32, low / len(cuts), high / len(cuts))
        loudness = loudness * jnp.repeat(jnp.exp(steps), shape[position] // shards_of).reshape((-1,) + (1,) * (len(shape) - 1 - position))
    return loudness


def noise(key, dims, width, limit, shards=(), kind=jnp.bfloat16):
    factor_of = shard_levels(key, dims, shards, -0.22, 0.18) if shards else 1.0
    result = jax.random.normal(key, dims, jnp.float32) * width * factor_of
    return jnp.minimum(jnp.maximum(result, -limit), limit).astype(kind)


def setup_inputs(seed: int = 0) -> dict:
    keys = jax.random.split(jax.random.key(seed), 10)
    return {
        "adjoint": noise(keys[0], (K, N_HARM, N_NODE * SUB), 1.0, 6.0, ((0, 4), (2, 8))),
        "source": noise(keys[1], (K, NODES), 1.0, 6.0, ((1, 32),), jnp.float32),
        "rad_coeff": jnp.clip(jnp.exp(math.log(2.0) - 2.306499 * jax.random.uniform(keys[2], (P_SIZE, NODES), jnp.float32) ** shard_levels(keys[2], (P_SIZE, NODES), ((1, 32),), -0.2, 0.2)), 0.19921875, 2.0).astype(jnp.bfloat16),
        "capacity": jnp.clip(jnp.exp(math.log(0.03) - 1.7917595 * jax.random.uniform(keys[3], (NODES,), jnp.float32) ** shard_levels(keys[3], (NODES,), ((0, 32),), -0.2, 0.2)), 0.005, 0.03),
        "inv_diag": jnp.clip(jnp.exp(math.log(0.5) - 1.609438 * jax.random.uniform(keys[4], (NODES,), jnp.float32) ** shard_levels(keys[4], (NODES,), ((0, 32),), -0.2, 0.2)), 0.1, 0.5),
        "blocks": noise(keys[5], (NBLK, NNZ, BLK, BLK), (BLK * NNZ) ** -0.5, 0.25, ((0, 32),)),
        "block_cols": draw_block_cols(jax.random.fold_in(keys[9], 71), 0),
        "zone_of": draw_zone_of(jax.random.fold_in(keys[9], 71), 0),
        "heater_weight": jnp.clip(jnp.exp(math.log(2.0) - 2.3025851 * jax.random.uniform(keys[8], (NODES,), jnp.float32) ** shard_levels(keys[8], (NODES,), ((0, 32),), -0.2, 0.2)), 0.2, 2.0),
    }


def fourier_basis(count):
    sample_index = jnp.arange(count, dtype=jnp.float32)[:, None]
    column_index = jnp.arange(count)[None, :]
    half_count = count // 2
    frequency = jnp.where(column_index <= half_count, column_index, column_index - half_count).astype(jnp.float32)
    angle = 2.0 * math.pi * frequency * sample_index / count
    values_table = jnp.where(column_index <= half_count, jnp.cos(angle), jnp.sin(angle))
    scaling = jnp.where((column_index == 0) | (column_index == half_count), math.sqrt(1.0 / count), math.sqrt(2.0 / count))
    return (values_table * scaling).astype(jnp.bfloat16)

def derivative_term(field):
    half_count = field.shape[0] // 2
    wave_number = jnp.arange(1, half_count, dtype=jnp.float32)[:, None]
    zero_row = jnp.zeros((1, field.shape[1]), jnp.float32)
    upper_rows = wave_number * field[half_count + 1:]
    lower_rows = -wave_number * field[1:half_count]
    return jnp.concatenate([zero_row, upper_rows, zero_row, lower_rows], axis=0)

def reference(adjoint, source, rad_coeff, capacity, inv_diag, blocks, block_cols, zone_of, heater_weight):
    adjoint_nodes = adjoint.reshape(K, NODES)
    fourier = fourier_basis(K)
    lam_blocks = adjoint_nodes.reshape(K, NBLK, BLK)
    groups = NODES // SUB

    def group_step(group):
        start = (group * SUB).astype(jnp.int32)
        field = lax.dynamic_slice_in_dim(adjoint_nodes, start, SUB, 1)
        samples = jnp.dot(fourier, field, preferred_element_type=jnp.float32)
        coeff_slice = lax.dynamic_slice_in_dim(rad_coeff, start, SUB, 1)
        weighted = (coeff_slice.astype(jnp.float32) * samples).astype(jnp.bfloat16)
        radiative = jnp.dot(fourier.T, weighted, preferred_element_type=jnp.float32)
        rate_term = derivative_term(field.astype(jnp.float32))
        block_start = (group * RB).astype(jnp.int32)
        col_slice = lax.dynamic_slice_in_dim(block_cols, block_start, RB, 0)
        block_slice = lax.dynamic_slice_in_dim(blocks, block_start, RB, 0)
        gathered = jnp.take(lam_blocks, col_slice, axis=1)
        conduction = jnp.einsum('kbsj,bsij->kbi', gathered.astype(jnp.float32), block_slice.astype(jnp.float32)).reshape(K, SUB)
        source_slice = lax.dynamic_slice_in_dim(source, start, SUB, 1)
        capacity_slice = lax.dynamic_slice_in_dim(capacity, start, SUB, 0)
        inverse_slice = lax.dynamic_slice_in_dim(inv_diag, start, SUB, 0)
        residual = source_slice - (capacity_slice[None, :] * rate_term + conduction + radiative)
        return (field.astype(jnp.float32) + inverse_slice[None, :] * residual).astype(jnp.bfloat16)
    pieces = lax.map(group_step, jnp.arange(groups, dtype=jnp.int32))
    updated_nodes = jnp.transpose(pieces, (1, 0, 2)).reshape(K, NODES)
    weighted_terms = (updated_nodes.astype(jnp.float32) * heater_weight[None, :]).T
    gradient = jax.ops.segment_sum(weighted_terms, zone_of, num_segments=ZONES)
    return (updated_nodes.reshape(K, N_HARM, N_NODE * SUB), gradient)
```

```python
import functools
import math

import jax
import jax.numpy as jnp
import numpy as np
from jax import lax
from jax.experimental import pallas as pl
from jax.experimental.pallas import tpu as pltpu
from jax.sharding import PartitionSpec as P

ZONE_DEV = 40
ROWS = 16
PARTS = 4
WIDTH = 256
TILES = 8
MESH = pl.DeviceIdType.MESH
NT = (((1,), (1,)), ((), ()))


def fourier_basis(count):
    sample_index = np.arange(count, dtype=np.float32)[:, None]
    column_index = np.arange(count)[None, :]
    half_count = count // 2
    frequency = np.where(
        column_index <= half_count, column_index, column_index - half_count
    ).astype(np.float32)
    angle = np.float32(2.0 * math.pi) * frequency * sample_index / np.float32(count)
    values_table = np.where(column_index <= half_count, np.cos(angle), np.sin(angle))
    scaling = np.where(
        (column_index == 0) | (column_index == half_count),
        math.sqrt(1.0 / count),
        math.sqrt(2.0 / count),
    ).astype(np.float32)
    return (values_table * scaling).astype(jnp.bfloat16)


def kernel(n_harm, n_node, n_chunk, *refs):
    (
        adj_any,
        src_any,
        rad_any,
        blk_any,
        capacity_any,
        inv_diag_any,
        weight_any,
        zone_any,
        cols_any,
        fourier_any,
        fourier_t_any,
        out,
        grad,
    ) = refs[:13]
    ext = refs[13 : 13 + n_chunk]
    (
        adj,
        src,
        rad,
        blk,
        capacity,
        inv_diag,
        weight,
        zone,
        cols,
        fourier,
        fourier_t,
        stage,
        sent,
        rate_k,
        upd,
        ret,
        select,
        part,
        from_prev,
        from_next,
        load_sem,
        adj_sem,
        own_in,
        in_send,
        in_recv,
        halo_send,
        halo_recv,
        direct_send,
        out_send,
        out_recv,
        own_out,
        part_send,
        part_recv,
    ) = refs[13 + n_chunk :]
    row_blocks = blk.shape[0]
    slots = blk.shape[1]
    nodes = row_blocks * 128
    per_part = row_blocks // PARTS
    chunk_rows = n_harm * ROWS
    me_h = lax.axis_index("harm")
    me_n = lax.axis_index("node")
    pos = me_h * n_node + me_n
    last = n_harm * n_node - 1
    last_n = n_node - 1
    mid = n_harm // 2
    has_prev = pos > 0
    has_next = pos < last
    prev = jnp.maximum(pos - 1, 0)
    following = jnp.minimum(pos + 1, last)
    prev_id = (prev // n_node, prev % n_node)
    next_id = (following // n_node, following % n_node)
    sides = ((has_prev, prev_id, 2), (has_next, next_id, 0))

    low_owner = (me_h == mid - 1) & (me_n == last_n)
    high_owner = (me_h == mid) & (me_n == 0)
    direct = (
        ((me_n == 0) & (me_h < mid), (mid - 1, last_n), mid, 2),
        ((me_n == last_n) & (me_h >= mid), (mid, 0), mid - 1, 0),
    )

    adj_loads = [
        pltpu.make_async_copy(
            adj_any.at[pl.ds(c * ROWS, ROWS)], adj.at[pl.ds(c * ROWS, ROWS)], adj_sem.at[c]
        )
        for c in range(n_chunk)
    ]
    loads = [
        pltpu.make_async_copy(there, here, load_sem.at[i])
        for i, (there, here) in enumerate(
            (
                (weight_any, weight),
                (zone_any, zone),
                (fourier_any, fourier),
                (fourier_t_any, fourier_t),
                (capacity_any, capacity),
                (inv_diag_any, inv_diag),
                (cols_any, cols),
                (rad_any, rad),
                (src_any, src),
                (blk_any, blk),
            )
        )
    ]
    for load in adj_loads:
        load.start()

    barrier = pltpu.get_barrier_semaphore()

    def greet(device):
        pl.semaphore_signal(barrier, inc=1, device_id=device, device_id_type=MESH)

    for d in range(1, n_harm):
        greet((lax.rem(me_h + d, n_harm), me_n))
    for there, device, _ in sides:
        pl.when(there)(functools.partial(greet, device))
    for there, device, _, _ in direct:
        pl.when(there)(functools.partial(greet, device))

    @pl.when(low_owner)
    def _():
        for h in range(mid):
            greet((h, 0))

    @pl.when(high_owner)
    def _():
        for h in range(mid, n_harm):
            greet((h, last_n))

    for load in loads:
        load.start()

    tile_rows = n_harm * ROWS

    def spread(c):
        def step(i, carry):
            at = pl.ds(pl.multiple_of(i * (TILES * 128), TILES * 128), TILES * 128)
            x = adj[c * ROWS : (c + 1) * ROWS, :, at]
            x = x.reshape(tile_rows, TILES * 128).astype(jnp.float32)
            for t in range(TILES):
                stage[t * tile_rows : (t + 1) * tile_rows, :] = x[:, t * 128 : (t + 1) * 128]
            for s in range(n_harm):
                for t in range(TILES):
                    rows = stage[pl.ds(t * tile_rows + s, ROWS, stride=n_harm), :]
                    sent[s, c, i * TILES + t] = rows.astype(jnp.bfloat16)
            return carry

        lax.fori_loop(0, row_blocks // TILES, step, 0)

    def of_part(p, start=0):
        return pl.ds(start + p * per_part, per_part)

    def arrive(d, c, p):
        peer = lax.rem(me_h + d, n_harm)
        return pltpu.make_async_remote_copy(
            src_ref=sent.at[peer, c, of_part(p)],
            dst_ref=ext[c].at[me_h, of_part(p, row_blocks)],
            send_sem=in_send.at[d, c, p],
            recv_sem=in_recv.at[d, c, p],
            device_id=(peer, me_n),
            device_id_type=MESH,
        )

    def own(c):
        return pltpu.make_async_copy(
            sent.at[me_h, c], ext[c].at[me_h, pl.ds(row_blocks, row_blocks)], own_in.at[c]
        )

    def halo(piece, c, p, side, mine=False):
        _, device, place = sides[side]
        if mine:
            source = sent.at[me_h, c, of_part(p)]
        else:
            source = ext[c].at[piece, of_part(p, row_blocks)]
        return pltpu.make_async_remote_copy(
            src_ref=source,
            dst_ref=ext[c].at[piece, of_part(p, place * row_blocks)],
            send_sem=halo_send.at[side, piece, c, p],
            recv_sem=halo_recv.at[side, piece, c, p],
            device_id=device,
            device_id_type=MESH,
        )

    def direct_halo(c, p, side):
        _, device, s, place = direct[side]
        return pltpu.make_async_remote_copy(
            src_ref=sent.at[s, c, of_part(p)],
            dst_ref=ext[c].at[me_h, of_part(p, place * row_blocks)],
            send_sem=direct_send.at[c, p],
            recv_sem=halo_recv.at[side, me_h, c, p],
            device_id=device,
            device_id_type=MESH,
        )

    def piece_of(d):
        return lax.rem(me_h - d + n_harm, n_harm)

    def forwards(d, side):
        piece = piece_of(d)
        if side == 0:
            return has_prev & jnp.logical_not(high_owner & (piece < mid))
        return has_next & jnp.logical_not(low_owner & (piece >= mid))

    def start_halo(d, c, p):
        for side in range(2):

            @pl.when(forwards(d, side))
            def _(side=side):
                halo(piece_of(d), c, p, side, mine=d == 0).start()

    order = sorted(range(1, n_harm), key=lambda d: abs(d - mid))

    def send(c):
        for p in range(PARTS):
            for d in order:
                arrive(d, c, p).start()
            start_halo(0, c, p)
            for side in range(2):

                @pl.when(direct[side][0])
                def _(side=side, p=p):
                    direct_halo(c, p, side).start()

        own(c).start()

    adj_loads[0].wait()
    spread(0)
    one = jnp.int32(1)
    zero = jnp.int32(0)
    expected = (
        jnp.int32(n_harm - 1)
        + jnp.where(has_prev, one, zero)
        + jnp.where(has_next, one, zero)
        + jnp.where(direct[0][0], one, zero)
        + jnp.where(direct[1][0], one, zero)
        + jnp.where(low_owner, jnp.int32(mid), zero)
        + jnp.where(high_owner, jnp.int32(n_harm - mid), zero)
    )
    pl.semaphore_wait(barrier, expected)
    send(0)
    for c in range(1, n_chunk):
        adj_loads[c].wait()
        spread(c)
        send(c)

    half = chunk_rows // 2
    for c in range(n_chunk):
        row = lax.broadcasted_iota(jnp.int32, (chunk_rows, 128), 0)
        k = (row // ROWS) * (n_chunk * ROWS) + c * ROWS + row % ROWS
        half_k = n_harm * n_chunk * ROWS // 2
        rate = jnp.where(k < half_k, k, half_k - k).astype(jnp.float32)
        rate_k[c * chunk_rows : (c + 1) * chunk_rows, :] = rate

    for load in loads:
        load.wait()

    zone_row = lax.broadcasted_iota(jnp.int32, (128, WIDTH), 0)

    def select_step(i, carry):
        at = pl.ds(pl.multiple_of(i * WIDTH, WIDTH), WIDTH)
        hit = zone_row == (zone[:, at] - (pos - 1) * ZONE_DEV)
        w = weight[:, at]
        high = w.astype(jnp.bfloat16).astype(jnp.float32)
        select[0:128, at] = jnp.where(hit, high, 0.0).astype(jnp.bfloat16)
        select[128:256, at] = jnp.where(hit, w - high, 0.0).astype(jnp.bfloat16)
        return carry

    lax.fori_loop(0, nodes // WIDTH, select_step, 0)

    def block_of(c, index):
        return jnp.concatenate([ext[c][h, index] for h in range(n_harm)], axis=0)

    def local_part(p):
        def local_step(i, carry):
            at = pl.ds(pl.multiple_of(i * WIDTH, WIDTH), WIDTH)
            first = row_blocks + i * (WIDTH // 128)
            pieces = [
                jnp.concatenate([block_of(c, first + t) for t in range(WIDTH // 128)], axis=1)
                for c in range(n_chunk)
            ]
            field = jnp.concatenate(pieces, axis=0) if n_chunk > 1 else pieces[0]
            samples = jnp.dot(fourier[...], field, preferred_element_type=jnp.float32)
            weighted = (rad[:, at].astype(jnp.float32) * samples).astype(jnp.bfloat16)
            radiative = jnp.dot(fourier_t[...], weighted, preferred_element_type=jnp.float32)
            cap = capacity[:, at]
            for c in range(n_chunk):
                lam = pieces[c].astype(jnp.float32)
                swapped = jnp.concatenate([lam[half:], lam[:half]], axis=0)
                rows = slice(c * chunk_rows, (c + 1) * chunk_rows)
                k = jnp.concatenate([rate_k[rows, :]] * (WIDTH // 128), axis=1)
                rate = k * swapped
                rest = src[:, c, :, at].reshape(chunk_rows, WIDTH) - (cap * rate + radiative[rows])
                src[:, c, :, at] = rest.reshape(n_harm, ROWS, WIDTH)
            return carry

        steps = nodes // PARTS // WIDTH
        lax.fori_loop(p * steps, (p + 1) * steps, local_step, 0)

    def back(d, c, p):
        peer = lax.rem(me_h + d, n_harm)
        return pltpu.make_async_remote_copy(
            src_ref=upd.at[peer, c, of_part(p)],
            dst_ref=ret.at[me_h, c, of_part(p)],
            send_sem=out_send.at[d, c, p],
            recv_sem=out_recv.at[d, c, p],
            device_id=(peer, me_n),
            device_id_type=MESH,
        )

    def own_back(c, p):
        return pltpu.make_async_copy(
            upd.at[me_h, c, of_part(p)], ret.at[me_h, c, of_part(p)], own_out.at[c, p]
        )

    def conduct(c, p):
        def block_step(i, carry):
            b = p * per_part + i
            at = pl.ds(pl.multiple_of(b * 128, 128), 128)
            lam = block_of(c, row_blocks + b)
            taken = [lam]
            for s in range(1, slots):
                col = cols[s, b] - (pos - 1) * row_blocks
                col = jnp.minimum(jnp.maximum(col, 0), 3 * row_blocks - 1)
                taken.append(block_of(c, col))
            conductance = jnp.concatenate([blk[b, s] for s in range(slots)], axis=1)
            conduction = lax.dot_general(
                jnp.concatenate(taken, axis=1),
                conductance,
                NT,
                preferred_element_type=jnp.float32,
            )
            residual = src[:, c, :, at].reshape(chunk_rows, 128) - conduction
            new = lam.astype(jnp.float32) + inv_diag[:, at] * residual
            upd[:, c, b] = new.astype(jnp.bfloat16).reshape(n_harm, ROWS, 128)
            return carry

        lax.fori_loop(0, per_part, block_step, 0, unroll=2)
        for d in order:
            back(d, c, p).start()
        own_back(c, p).start()

    def wait_halo(c):
        for side in range(2):

            @pl.when(sides[1 - side][0])
            def _(side=side):
                for p in range(PARTS):
                    for piece in range(n_harm):
                        halo(piece, c, p, side).wait_recv()

    for c in range(n_chunk):
        own(c).wait()
        for p in range(PARTS):
            for d in range(1, n_harm):
                arrive(d, c, p).wait_recv()
                start_halo(d, c, p)
            if c == n_chunk - 1:
                local_part(p)

    for c in range(n_chunk):
        wait_halo(c)
        for p in range(PARTS):
            conduct(c, p)

    part[...] = jnp.zeros_like(part)
    wide = 512 // 128

    def gradient_step(i, carry):
        at = pl.ds(pl.multiple_of(i * 512, 512), 512)
        new = jnp.concatenate(
            [
                upd[:, :, i * wide + t].reshape(n_harm * n_chunk * ROWS, 128)
                for t in range(wide)
            ],
            axis=1,
        )
        both = lax.dot_general(select[:, at], new, NT, preferred_element_type=jnp.float32)
        part[...] += both[0:128] + both[128:256]
        return carry

    lax.fori_loop(0, nodes // 512, gradient_step, 0)

    def hand_over(side):
        _, device, place = sides[side]
        rows = pl.ds(0 if side == 0 else 2 * ZONE_DEV, ZONE_DEV)
        return pltpu.make_async_remote_copy(
            src_ref=part.at[rows, :],
            dst_ref=from_next if side == 0 else from_prev,
            send_sem=part_send.at[side],
            recv_sem=part_recv.at[side],
            device_id=device,
            device_id_type=MESH,
        )

    for side in range(2):

        @pl.when(sides[side][0])
        def _(side=side):
            hand_over(side).start()

    grad[...] = part[ZONE_DEV : 2 * ZONE_DEV, :]

    for side, buffer in ((0, from_next), (1, from_prev)):

        @pl.when(sides[1 - side][0])
        def _(side=side, buffer=buffer):
            hand_over(side).wait_recv()
            grad[...] += buffer[...]

    def gather(c, p):
        def step(i, carry):
            b = p * per_part + i * TILES
            at = pl.ds(pl.multiple_of(b * 128, 128), TILES * 128)
            for s in range(n_harm):
                for t in range(TILES):
                    stage[pl.ds(t * tile_rows + s, ROWS, stride=n_harm), :] = ret[
                        s, c, b + t
                    ].astype(jnp.float32)
            x = jnp.concatenate(
                [stage[t * tile_rows : (t + 1) * tile_rows, :] for t in range(TILES)], axis=1
            )
            x = x.astype(jnp.bfloat16).reshape(ROWS, n_harm, TILES * 128)
            out[c * ROWS : (c + 1) * ROWS, :, at] = x
            return carry

        lax.fori_loop(0, per_part // TILES, step, 0)

    for c in range(n_chunk):
        for p in range(PARTS):
            own_back(c, p).wait()
            for d in range(1, n_harm):
                back(d, c, p).wait_recv()
            gather(c, p)

    for c in range(n_chunk):
        for p in range(PARTS):
            for d in range(1, n_harm):
                arrive(d, c, p).wait_send()
                back(d, c, p).wait_send()
            for side in range(2):

                @pl.when(direct[side][0])
                def _(side=side, c=c, p=p):
                    direct_halo(c, p, side).wait_send()

                for d in range(n_harm):

                    @pl.when(forwards(d, side))
                    def _(side=side, d=d, c=c, p=p):
                        halo(piece_of(d), c, p, side, mine=d == 0).wait_send()

    for side in range(2):

        @pl.when(sides[side][0])
        def _(side=side):
            hand_over(side).wait_send()


def body(
    n_harm,
    n_node,
    adjoint,
    source,
    rad_coeff,
    capacity,
    inv_diag,
    blocks,
    block_cols,
    zone_of,
    heater_weight,
):
    rows, _, nodes = adjoint.shape
    n_chunk = rows // ROWS
    harmonics = n_harm * rows
    order = np.arange(harmonics).reshape(n_harm, n_chunk, ROWS).transpose(1, 0, 2).reshape(-1)
    basis = fourier_basis(harmonics)

    row_blocks = nodes // 128
    vmem = pl.BlockSpec(memory_space=pltpu.VMEM)
    hbm = pl.BlockSpec(memory_space=pltpu.HBM)
    piece = (n_harm, n_chunk, ROWS, nodes)
    tiles = (n_harm, n_chunk, row_blocks, ROWS, 128)
    line = (1, nodes)
    dma = pltpu.SemaphoreType.DMA
    updated, gradient = pl.pallas_call(
        functools.partial(kernel, n_harm, n_node, n_chunk),
        out_shape=(
            jax.ShapeDtypeStruct(adjoint.shape, jnp.bfloat16),
            jax.ShapeDtypeStruct((ZONE_DEV, harmonics), jnp.float32),
        ),
        in_specs=[hbm] * 11,
        out_specs=(vmem, vmem),
        scratch_shapes=[pltpu.VMEM((n_harm, 3 * row_blocks, ROWS, 128), jnp.bfloat16)] * n_chunk
        + [
            pltpu.VMEM(adjoint.shape, jnp.bfloat16),
            pltpu.VMEM(piece, jnp.float32),
            pltpu.VMEM(rad_coeff.shape, jnp.bfloat16),
            pltpu.VMEM(blocks.shape, jnp.bfloat16),
            pltpu.VMEM(line, jnp.float32),
            pltpu.VMEM(line, jnp.float32),
            pltpu.VMEM(line, jnp.float32),
            pltpu.VMEM(line, jnp.int32),
            pltpu.SMEM(block_cols.shape[::-1], jnp.int32),
            pltpu.VMEM((harmonics, harmonics), jnp.bfloat16),
            pltpu.VMEM((harmonics, harmonics), jnp.bfloat16),
            pltpu.VMEM((TILES * n_harm * ROWS, 128), jnp.float32),
            pltpu.VMEM(tiles, jnp.bfloat16),
            pltpu.VMEM((harmonics, 128), jnp.float32),
            pltpu.VMEM(tiles, jnp.bfloat16),
            pltpu.VMEM(tiles, jnp.bfloat16),
            pltpu.VMEM((256, nodes), jnp.bfloat16),
            pltpu.VMEM((128, harmonics), jnp.float32),
            pltpu.VMEM((ZONE_DEV, harmonics), jnp.float32),
            pltpu.VMEM((ZONE_DEV, harmonics), jnp.float32),
            dma((10,)),
            dma((n_chunk,)),
            dma((n_chunk,)),
            dma((n_harm, n_chunk, PARTS)),
            dma((n_harm, n_chunk, PARTS)),
            dma((2, n_harm, n_chunk, PARTS)),
            dma((2, n_harm, n_chunk, PARTS)),
            dma((n_chunk, PARTS)),
            dma((n_harm, n_chunk, PARTS)),
            dma((n_harm, n_chunk, PARTS)),
            dma((n_chunk, PARTS)),
            dma((2,)),
            dma((2,)),
        ],
        compiler_params=pltpu.CompilerParams(
            collective_id=0, has_side_effects=True, vmem_limit_bytes=48 * 2**20
        ),
    )(
        *(
            pltpu.with_memory_space_constraint(x, pltpu.HBM)
            for x in (
                adjoint,
                source.reshape(piece),
                rad_coeff,
                blocks,
                capacity[None, :],
                inv_diag[None, :],
                heater_weight[None, :],
                zone_of[None, :],
                block_cols.T,
                jnp.asarray(basis[:, order]),
                jnp.asarray(basis.T[order]),
            )
        )
    )
    return updated, gradient


def solution(mesh):
    in_specs = (
        P("harm", None, "node"),
        P(None, ("harm", "node")),
        P(None, ("harm", "node")),
        P(("harm", "node")),
        P(("harm", "node")),
        P(("harm", "node"), None, None, None),
        P(("harm", "node"), None),
        P(("harm", "node")),
        P(("harm", "node")),
    )
    out_specs = (P("harm", None, "node"), P(("harm", "node"), None))
    step = functools.partial(body, mesh.shape["harm"], mesh.shape["node"])
    return jax.shard_map(step, mesh=mesh, in_specs=in_specs, out_specs=out_specs, check_vma=False)
```

```python
import functools
import math

import jax
import jax.numpy as jnp
import numpy as np
from jax import lax
from jax.experimental import pallas as pl
from jax.experimental.pallas import tpu as pltpu
from jax.sharding import PartitionSpec as P

ZONE_DEV = 40
ROWS = 16
PARTS = 4
EARLY = 0
LAG = 0
WIDTH = 256
TILES = 8
MESH = pl.DeviceIdType.MESH
NT = (((1,), (1,)), ((), ()))


def fourier_basis(count):
    sample_index = np.arange(count, dtype=np.float32)[:, None]
    column_index = np.arange(count)[None, :]
    half_count = count // 2
    frequency = np.where(
        column_index <= half_count, column_index, column_index - half_count
    ).astype(np.float32)
    angle = np.float32(2.0 * math.pi) * frequency * sample_index / np.float32(count)
    values_table = np.where(column_index <= half_count, np.cos(angle), np.sin(angle))
    scaling = np.where(
        (column_index == 0) | (column_index == half_count),
        math.sqrt(1.0 / count),
        math.sqrt(2.0 / count),
    ).astype(np.float32)
    return (values_table * scaling).astype(jnp.bfloat16)


def kernel(n_harm, n_node, n_chunk, *refs):
    (
        adj_any,
        src_any,
        rad_any,
        blk_any,
        capacity_any,
        inv_diag_any,
        weight_any,
        zone_any,
        cols_any,
        fourier_any,
        fourier_t_any,
        out,
        grad,
    ) = refs[:13]
    ext = refs[13 : 13 + n_chunk]
    (
        adj,
        src,
        rad,
        blk,
        capacity,
        inv_diag,
        weight,
        zone,
        cols,
        fourier,
        fourier_t,
        stage,
        sent,
        rate_k,
        upd,
        ret,
        select,
        part,
        from_prev,
        from_next,
        load_sem,
        adj_sem,
        own_in,
        in_send,
        in_recv,
        halo_send,
        halo_recv,
        direct_send,
        out_send,
        out_recv,
        own_out,
        part_send,
        part_recv,
        held,
        depart_send,
        bend_send,
        bend_recv,
    ) = refs[13 + n_chunk :]
    row_blocks = blk.shape[0]
    slots = blk.shape[1]
    nodes = row_blocks * 128
    per_part = row_blocks // PARTS
    chunk_rows = n_harm * ROWS
    me_h = lax.axis_index("harm")
    me_n = lax.axis_index("node")
    pos = me_h * n_node + me_n
    last = n_harm * n_node - 1
    last_n = n_node - 1
    mid = n_harm // 2
    has_prev = pos > 0
    has_next = pos < last
    prev = jnp.maximum(pos - 1, 0)
    following = jnp.minimum(pos + 1, last)
    prev_id = (prev // n_node, prev % n_node)
    next_id = (following // n_node, following % n_node)
    sides = ((has_prev, prev_id, 2), (has_next, next_id, 0))

    at_first = me_n == 0
    at_last = me_n == last_n

    def straight(h, other):
        return jnp.equal(jnp.greater_equal(h, mid), jnp.greater_equal(other, mid))

    direct = [
        [
            (at_first & straight(me_h, t - 1), (t - 1, last_n), t, 2),
            (at_last & straight(me_h, t), (t, 0), t - 1, 0),
        ]
        for t in range(1, n_harm)
    ]
    greeted = [(there, device) for there, device, _ in sides]
    greeted += [(there, device) for pair in direct for there, device, _, _ in pair]
    for h in range(n_harm):
        greeted.append((at_first & (me_h > 0) & straight(h, me_h), (h, last_n)))
        greeted.append((at_last & (me_h < n_harm - 1) & straight(h, me_h), (h, 0)))

    low = me_h < mid
    high = me_h >= mid
    origin = (at_first & high, at_last & low)
    goal = ((mid - 1, last_n), (mid, 0))
    at_goal = ((me_h == mid - 1) & at_last, (me_h == mid) & at_first)
    group = (mid, mid - 1)
    far = (range(mid, n_harm), range(mid))
    start_n = (0, last_n)

    def way_n(p, side):
        step = 2 * (p % (n_node // 2))
        return last_n - step if side else step

    def at_way(p, side):
        return (low if side else high) & (me_n == way_n(p, side))

    bends = [
        (p, side) for p in range(PARTS) for side in range(2) if way_n(p, side) != start_n[side]
    ]
    for side in range(2):
        for n in sorted({way_n(p, side) for p in range(PARTS)}):
            greeted += [(at_goal[side], (h, n)) for h in far[side]]
            here = (low if side else high) & (me_n == n)
            greeted.append((here, goal[side]))
            if n != start_n[side]:
                greeted.append((here, (me_h, start_n[side])))
                greeted.append((origin[side], (me_h, n)))

    adj_loads = [
        pltpu.make_async_copy(
            adj_any.at[pl.ds(c * ROWS, ROWS)], adj.at[pl.ds(c * ROWS, ROWS)], adj_sem.at[c]
        )
        for c in range(n_chunk)
    ]
    loads = [
        pltpu.make_async_copy(there, here, load_sem.at[i])
        for i, (there, here) in enumerate(
            (
                (weight_any, weight),
                (zone_any, zone),
                (fourier_any, fourier),
                (fourier_t_any, fourier_t),
                (capacity_any, capacity),
                (inv_diag_any, inv_diag),
                (cols_any, cols),
                (rad_any, rad),
                (src_any, src),
                (blk_any, blk),
            )
        )
    ]
    for load in adj_loads:
        load.start()

    barrier = pltpu.get_barrier_semaphore()

    def greet(device):
        pl.semaphore_signal(barrier, inc=1, device_id=device, device_id_type=MESH)

    for d in range(1, n_harm):
        greet((lax.rem(me_h + d, n_harm), me_n))
    for there, device in greeted:
        pl.when(there)(functools.partial(greet, device))

    for load in loads:
        load.start()

    tile_rows = n_harm * ROWS

    def spread(c):
        def step(i, carry):
            at = pl.ds(pl.multiple_of(i * (TILES * 128), TILES * 128), TILES * 128)
            x = adj[c * ROWS : (c + 1) * ROWS, :, at]
            x = x.reshape(tile_rows, TILES * 128).astype(jnp.float32)
            for t in range(TILES):
                stage[t * tile_rows : (t + 1) * tile_rows, :] = x[:, t * 128 : (t + 1) * 128]
            for s in range(n_harm):
                for t in range(TILES):
                    rows = stage[pl.ds(t * tile_rows + s, ROWS, stride=n_harm), :]
                    sent[s, c, i * TILES + t] = rows.astype(jnp.bfloat16)
            return carry

        lax.fori_loop(0, row_blocks // TILES, step, 0)

    def of_part(p, start=0):
        return pl.ds(start + p * per_part, per_part)

    def arrive(d, c, p):
        peer = lax.rem(me_h + d, n_harm)
        return pltpu.make_async_remote_copy(
            src_ref=sent.at[peer, c, of_part(p)],
            dst_ref=ext[c].at[me_h, of_part(p, row_blocks)],
            send_sem=in_send.at[d, c, p],
            recv_sem=in_recv.at[d, c, p],
            device_id=(peer, me_n),
            device_id_type=MESH,
        )

    def own(c):
        return pltpu.make_async_copy(
            sent.at[me_h, c], ext[c].at[me_h, pl.ds(row_blocks, row_blocks)], own_in.at[c]
        )

    def halo(piece, c, p, side, mine=False):
        _, device, place = sides[side]
        if mine:
            source = sent.at[me_h, c, of_part(p)]
        else:
            source = ext[c].at[piece, of_part(p, row_blocks)]
        return pltpu.make_async_remote_copy(
            src_ref=source,
            dst_ref=ext[c].at[piece, of_part(p, place * row_blocks)],
            send_sem=halo_send.at[side, piece, c, p],
            recv_sem=halo_recv.at[side, piece, c, p],
            device_id=device,
            device_id_type=MESH,
        )

    def direct_halo(c, p, t, side):
        _, device, s, place = direct[t][side]
        return pltpu.make_async_remote_copy(
            src_ref=sent.at[s, c, of_part(p)],
            dst_ref=ext[c].at[me_h, of_part(p, place * row_blocks)],
            send_sem=direct_send.at[t, c, p],
            recv_sem=halo_recv.at[side, me_h, c, p],
            device_id=device,
            device_id_type=MESH,
        )

    def depart(c, p, side):
        bent = (p, side) in bends
        if bent:
            landing, done = held.at[p, c], bend_recv.at[p, c]
        else:
            landing = ext[c].at[me_h, of_part(p, sides[side][2] * row_blocks)]
            done = halo_recv.at[side, me_h, c, p]
        return pltpu.make_async_remote_copy(
            src_ref=sent.at[group[side], c, of_part(p)],
            dst_ref=landing,
            send_sem=depart_send.at[c, p],
            recv_sem=done,
            device_id=(me_h, way_n(p, side)) if bent else goal[side],
            device_id_type=MESH,
        )

    def relay_on(c, p, side):
        return pltpu.make_async_remote_copy(
            src_ref=held.at[p, c],
            dst_ref=ext[c].at[me_h, of_part(p, sides[side][2] * row_blocks)],
            send_sem=bend_send.at[p, c],
            recv_sem=halo_recv.at[side, me_h, c, p],
            device_id=goal[side],
            device_id_type=MESH,
        )

    def relay(c):
        for p, side in bends:

            @pl.when(at_way(p, side))
            def _(p=p, side=side):
                depart(c, p, side).wait_recv()
                relay_on(c, p, side).start()

    def piece_of(d):
        return lax.rem(me_h - d + n_harm, n_harm)

    def forwards(d, side):
        piece = piece_of(d)
        if side == 0:
            skip = straight(piece, me_h - 1) | (me_h == mid)
            return has_prev & jnp.logical_not(at_first & skip)
        skip = straight(piece, me_h + 1) | (me_h + 1 == mid)
        return has_next & jnp.logical_not(at_last & skip)

    def start_halo(d, c, p):
        for side in range(2):

            @pl.when(forwards(d, side))
            def _(side=side):
                halo(piece_of(d), c, p, side, mine=d == 0).start()

    order = sorted(range(1, n_harm), key=lambda d: abs(d - mid))

    def send(c):
        for side in range(2):

            @pl.when(origin[side])
            def _(side=side):
                for p in range(PARTS):
                    depart(c, p, side).start()

        for p in range(PARTS):
            for d in order:
                arrive(d, c, p).start()
            start_halo(0, c, p)
            for t in range(n_harm - 1):
                for side in range(2):

                    @pl.when(direct[t][side][0])
                    def _(t=t, side=side, p=p):
                        direct_halo(c, p, t, side).start()

        own(c).start()

    adj_loads[0].wait()
    spread(0)
    expected = jnp.int32(n_harm - 1)
    for there, _ in greeted:
        expected = expected + jnp.where(there, jnp.int32(1), jnp.int32(0))
    pl.semaphore_wait(barrier, expected)
    send(0)
    for c in range(1, n_chunk):
        adj_loads[c].wait()
        spread(c)
        relay(c - 1)
        send(c)

    half = chunk_rows // 2
    for c in range(n_chunk):
        row = lax.broadcasted_iota(jnp.int32, (chunk_rows, 128), 0)
        k = (row // ROWS) * (n_chunk * ROWS) + c * ROWS + row % ROWS
        half_k = n_harm * n_chunk * ROWS // 2
        rate = jnp.where(k < half_k, k, half_k - k).astype(jnp.float32)
        rate_k[c * chunk_rows : (c + 1) * chunk_rows, :] = rate

    for load in loads:
        load.wait()

    zone_row = lax.broadcasted_iota(jnp.int32, (128, WIDTH), 0)

    def select_step(i, carry):
        at = pl.ds(pl.multiple_of(i * WIDTH, WIDTH), WIDTH)
        hit = zone_row == (zone[:, at] - (pos - 1) * ZONE_DEV)
        w = weight[:, at]
        high = w.astype(jnp.bfloat16).astype(jnp.float32)
        select[0:128, at] = jnp.where(hit, high, 0.0).astype(jnp.bfloat16)
        select[128:256, at] = jnp.where(hit, w - high, 0.0).astype(jnp.bfloat16)
        return carry

    lax.fori_loop(0, nodes // WIDTH, select_step, 0)
    relay(n_chunk - 1)

    def block_of(c, index):
        return jnp.concatenate([ext[c][h, index] for h in range(n_harm)], axis=0)

    def local_part(p):
        def local_step(i, carry):
            at = pl.ds(pl.multiple_of(i * WIDTH, WIDTH), WIDTH)
            first = row_blocks + i * (WIDTH // 128)
            pieces = [
                jnp.concatenate([block_of(c, first + t) for t in range(WIDTH // 128)], axis=1)
                for c in range(n_chunk)
            ]
            field = jnp.concatenate(pieces, axis=0) if n_chunk > 1 else pieces[0]
            samples = jnp.dot(fourier[...], field, preferred_element_type=jnp.float32)
            weighted = (rad[:, at].astype(jnp.float32) * samples).astype(jnp.bfloat16)
            radiative = jnp.dot(fourier_t[...], weighted, preferred_element_type=jnp.float32)
            cap = capacity[:, at]
            for c in range(n_chunk):
                lam = pieces[c].astype(jnp.float32)
                swapped = jnp.concatenate([lam[half:], lam[:half]], axis=0)
                rows = slice(c * chunk_rows, (c + 1) * chunk_rows)
                k = jnp.concatenate([rate_k[rows, :]] * (WIDTH // 128), axis=1)
                rate = k * swapped
                rest = src[:, c, :, at].reshape(chunk_rows, WIDTH) - (cap * rate + radiative[rows])
                src[:, c, :, at] = rest.reshape(n_harm, ROWS, WIDTH)
            return carry

        steps = nodes // PARTS // WIDTH
        lax.fori_loop(p * steps, (p + 1) * steps, local_step, 0)

    def back(d, c, p):
        peer = lax.rem(me_h + d, n_harm)
        return pltpu.make_async_remote_copy(
            src_ref=upd.at[peer, c, of_part(p)],
            dst_ref=ret.at[me_h, c, of_part(p)],
            send_sem=out_send.at[d, c, p],
            recv_sem=out_recv.at[d, c, p],
            device_id=(peer, me_n),
            device_id_type=MESH,
        )

    def own_back(c, p):
        return pltpu.make_async_copy(
            upd.at[me_h, c, of_part(p)], ret.at[me_h, c, of_part(p)], own_out.at[c, p]
        )

    def conduct(c, p):
        def block_step(i, carry):
            b = p * per_part + i
            at = pl.ds(pl.multiple_of(b * 128, 128), 128)
            lam = block_of(c, row_blocks + b)
            taken = [lam]
            for s in range(1, slots):
                col = cols[s, b] - (pos - 1) * row_blocks
                col = jnp.minimum(jnp.maximum(col, 0), 3 * row_blocks - 1)
                taken.append(block_of(c, col))
            conductance = jnp.concatenate([blk[b, s] for s in range(slots)], axis=1)
            conduction = lax.dot_general(
                jnp.concatenate(taken, axis=1),
                conductance,
                NT,
                preferred_element_type=jnp.float32,
            )
            residual = src[:, c, :, at].reshape(chunk_rows, 128) - conduction
            new = lam.astype(jnp.float32) + inv_diag[:, at] * residual
            upd[:, c, b] = new.astype(jnp.bfloat16).reshape(n_harm, ROWS, 128)
            return carry

        lax.fori_loop(0, per_part, block_step, 0, unroll=2)
        for d in order:
            back(d, c, p).start()
        own_back(c, p).start()

    def wait_halo(c):
        for side in range(2):

            @pl.when(sides[1 - side][0])
            def _(side=side):
                for p in range(PARTS):
                    for piece in range(n_harm):
                        halo(piece, c, p, side).wait_recv()

    def take(c, p):
        if p == 0:
            own(c).wait()
        for d in range(1, n_harm):
            arrive(d, c, p).wait_recv()
            start_halo(d, c, p)

    final = n_chunk - 1
    for c in range(final):
        for p in range(PARTS):
            take(c, p)
    done = 0
    for p in range(PARTS):
        take(final, p)
        local_part(p)
        if final > 0 and p >= EARLY:
            if done == 0:
                wait_halo(0)
            while done < p - LAG + 1:
                conduct(0, done)
                done += 1
    for c in range(n_chunk):
        if c > 0 or done == 0:
            wait_halo(c)
        for p in range(done if c == 0 else 0, PARTS):
            conduct(c, p)

    part[...] = jnp.zeros_like(part)
    wide = 512 // 128

    def gradient_step(i, carry):
        at = pl.ds(pl.multiple_of(i * 512, 512), 512)
        new = jnp.concatenate(
            [
                upd[:, :, i * wide + t].reshape(n_harm * n_chunk * ROWS, 128)
                for t in range(wide)
            ],
            axis=1,
        )
        both = lax.dot_general(select[:, at], new, NT, preferred_element_type=jnp.float32)
        part[...] += both[0:128] + both[128:256]
        return carry

    lax.fori_loop(0, nodes // 512, gradient_step, 0)

    def hand_over(side):
        _, device, place = sides[side]
        rows = pl.ds(0 if side == 0 else 2 * ZONE_DEV, ZONE_DEV)
        return pltpu.make_async_remote_copy(
            src_ref=part.at[rows, :],
            dst_ref=from_next if side == 0 else from_prev,
            send_sem=part_send.at[side],
            recv_sem=part_recv.at[side],
            device_id=device,
            device_id_type=MESH,
        )

    for side in range(2):

        @pl.when(sides[side][0])
        def _(side=side):
            hand_over(side).start()

    grad[...] = part[ZONE_DEV : 2 * ZONE_DEV, :]

    for side, buffer in ((0, from_next), (1, from_prev)):

        @pl.when(sides[1 - side][0])
        def _(side=side, buffer=buffer):
            hand_over(side).wait_recv()
            grad[...] += buffer[...]

    def gather(c, p):
        def step(i, carry):
            b = p * per_part + i * TILES
            at = pl.ds(pl.multiple_of(b * 128, 128), TILES * 128)
            for s in range(n_harm):
                for t in range(TILES):
                    stage[pl.ds(t * tile_rows + s, ROWS, stride=n_harm), :] = ret[
                        s, c, b + t
                    ].astype(jnp.float32)
            x = jnp.concatenate(
                [stage[t * tile_rows : (t + 1) * tile_rows, :] for t in range(TILES)], axis=1
            )
            x = x.astype(jnp.bfloat16).reshape(ROWS, n_harm, TILES * 128)
            out[c * ROWS : (c + 1) * ROWS, :, at] = x
            return carry

        lax.fori_loop(0, per_part // TILES, step, 0)

    for c in range(n_chunk):
        for p in range(PARTS):
            own_back(c, p).wait()
            for d in range(1, n_harm):
                back(d, c, p).wait_recv()
            gather(c, p)

    for c in range(n_chunk):
        for p in range(PARTS):
            for d in range(1, n_harm):
                arrive(d, c, p).wait_send()
                back(d, c, p).wait_send()
            for side in range(2):
                for t in range(n_harm - 1):

                    @pl.when(direct[t][side][0])
                    def _(t=t, side=side, c=c, p=p):
                        direct_halo(c, p, t, side).wait_send()

                for d in range(n_harm):

                    @pl.when(forwards(d, side))
                    def _(side=side, d=d, c=c, p=p):
                        halo(piece_of(d), c, p, side, mine=d == 0).wait_send()

    for c in range(n_chunk):
        for side in range(2):

            @pl.when(origin[side])
            def _(c=c, side=side):
                for p in range(PARTS):
                    depart(c, p, side).wait_send()

        for p, side in bends:

            @pl.when(at_way(p, side))
            def _(c=c, p=p, side=side):
                relay_on(c, p, side).wait_send()

    for side in range(2):

        @pl.when(sides[side][0])
        def _(side=side):
            hand_over(side).wait_send()


def body(
    n_harm,
    n_node,
    adjoint,
    source,
    rad_coeff,
    capacity,
    inv_diag,
    blocks,
    block_cols,
    zone_of,
    heater_weight,
):
    rows, _, nodes = adjoint.shape
    n_chunk = rows // ROWS
    harmonics = n_harm * rows
    order = np.arange(harmonics).reshape(n_harm, n_chunk, ROWS).transpose(1, 0, 2).reshape(-1)
    basis = fourier_basis(harmonics)

    row_blocks = nodes // 128
    vmem = pl.BlockSpec(memory_space=pltpu.VMEM)
    hbm = pl.BlockSpec(memory_space=pltpu.HBM)
    piece = (n_harm, n_chunk, ROWS, nodes)
    tiles = (n_harm, n_chunk, row_blocks, ROWS, 128)
    line = (1, nodes)
    dma = pltpu.SemaphoreType.DMA
    updated, gradient = pl.pallas_call(
        functools.partial(kernel, n_harm, n_node, n_chunk),
        out_shape=(
            jax.ShapeDtypeStruct(adjoint.shape, jnp.bfloat16),
            jax.ShapeDtypeStruct((ZONE_DEV, harmonics), jnp.float32),
        ),
        in_specs=[hbm] * 11,
        out_specs=(vmem, vmem),
        scratch_shapes=[pltpu.VMEM((n_harm, 3 * row_blocks, ROWS, 128), jnp.bfloat16)] * n_chunk
        + [
            pltpu.VMEM(adjoint.shape, jnp.bfloat16),
            pltpu.VMEM(piece, jnp.float32),
            pltpu.VMEM(rad_coeff.shape, jnp.bfloat16),
            pltpu.VMEM(blocks.shape, jnp.bfloat16),
            pltpu.VMEM(line, jnp.float32),
            pltpu.VMEM(line, jnp.float32),
            pltpu.VMEM(line, jnp.float32),
            pltpu.VMEM(line, jnp.int32),
            pltpu.SMEM(block_cols.shape[::-1], jnp.int32),
            pltpu.VMEM((harmonics, harmonics), jnp.bfloat16),
            pltpu.VMEM((harmonics, harmonics), jnp.bfloat16),
            pltpu.VMEM((TILES * n_harm * ROWS, 128), jnp.float32),
            pltpu.VMEM(tiles, jnp.bfloat16),
            pltpu.VMEM((harmonics, 128), jnp.float32),
            pltpu.VMEM(tiles, jnp.bfloat16),
            pltpu.VMEM(tiles, jnp.bfloat16),
            pltpu.VMEM((256, nodes), jnp.bfloat16),
            pltpu.VMEM((128, harmonics), jnp.float32),
            pltpu.VMEM((ZONE_DEV, harmonics), jnp.float32),
            pltpu.VMEM((ZONE_DEV, harmonics), jnp.float32),
            dma((10,)),
            dma((n_chunk,)),
            dma((n_chunk,)),
            dma((n_harm, n_chunk, PARTS)),
            dma((n_harm, n_chunk, PARTS)),
            dma((2, n_harm, n_chunk, PARTS)),
            dma((2, n_harm, n_chunk, PARTS)),
            dma((n_harm - 1, n_chunk, PARTS)),
            dma((n_harm, n_chunk, PARTS)),
            dma((n_harm, n_chunk, PARTS)),
            dma((n_chunk, PARTS)),
            dma((2,)),
            dma((2,)),
            pltpu.VMEM((PARTS, n_chunk, row_blocks // PARTS, ROWS, 128), jnp.bfloat16),
            dma((n_chunk, PARTS)),
            dma((PARTS, n_chunk)),
            dma((PARTS, n_chunk)),
        ],
        compiler_params=pltpu.CompilerParams(
            collective_id=0, has_side_effects=True, vmem_limit_bytes=48 * 2**20
        ),
    )(
        *(
            pltpu.with_memory_space_constraint(x, pltpu.HBM)
            for x in (
                adjoint,
                source.reshape(piece),
                rad_coeff,
                blocks,
                capacity[None, :],
                inv_diag[None, :],
                heater_weight[None, :],
                zone_of[None, :],
                block_cols.T,
                jnp.asarray(basis[:, order]),
                jnp.asarray(basis.T[order]),
            )
        )
    )
    return updated, gradient


def solution(mesh):
    in_specs = (
        P("harm", None, "node"),
        P(None, ("harm", "node")),
        P(None, ("harm", "node")),
        P(("harm", "node")),
        P(("harm", "node")),
        P(("harm", "node"), None, None, None),
        P(("harm", "node"), None),
        P(("harm", "node")),
        P(("harm", "node")),
    )
    out_specs = (P("harm", None, "node"), P(("harm", "node"), None))
    step = functools.partial(body, mesh.shape["harm"], mesh.shape["node"])
    return jax.shard_map(step, mesh=mesh, in_specs=in_specs, out_specs=out_specs, check_vma=False)
```

```python
import functools
import math

import jax
import jax.numpy as jnp
import numpy as np
from jax import lax
from jax.experimental import pallas as pl
from jax.experimental.pallas import tpu as pltpu
from jax.sharding import PartitionSpec as P

ZONE_DEV = 40
ROWS = 16
PARTS = 4
MAJOR = ()
ORDER = [3, 2, 1]
BACK = [2, 1, 3]
SLICES = 4
EARLY = 0
LAG = 0
WIDTH = 256
TILES = 8
MESH = pl.DeviceIdType.MESH
NT = (((1,), (1,)), ((), ()))


def fourier_basis(count):
    sample_index = np.arange(count, dtype=np.float32)[:, None]
    column_index = np.arange(count)[None, :]
    half_count = count // 2
    frequency = np.where(
        column_index <= half_count, column_index, column_index - half_count
    ).astype(np.float32)
    angle = np.float32(2.0 * math.pi) * frequency * sample_index / np.float32(count)
    values_table = np.where(column_index <= half_count, np.cos(angle), np.sin(angle))
    scaling = np.where(
        (column_index == 0) | (column_index == half_count),
        math.sqrt(1.0 / count),
        math.sqrt(2.0 / count),
    ).astype(np.float32)
    return (values_table * scaling).astype(jnp.bfloat16)


def kernel(n_harm, n_node, n_chunk, *refs):
    (
        adj_any,
        src_any,
        rad_any,
        blk_any,
        capacity_any,
        inv_diag_any,
        weight_any,
        zone_any,
        cols_any,
        fourier_any,
        fourier_t_any,
        out,
        grad,
    ) = refs[:13]
    ext = refs[13 : 13 + n_chunk]
    (
        adj,
        src,
        rad,
        blk,
        capacity,
        inv_diag,
        weight,
        zone,
        cols,
        fourier,
        fourier_t,
        stage,
        sent,
        rate_k,
        upd,
        ret,
        select,
        part,
        from_prev,
        from_next,
        load_sem,
        adj_sem,
        own_in,
        in_send,
        in_recv,
        halo_send,
        halo_recv,
        direct_send,
        out_send,
        out_recv,
        own_out,
        part_send,
        part_recv,
        held,
        depart_send,
        bend_send,
        bend_recv,
    ) = refs[13 + n_chunk :]
    row_blocks = blk.shape[0]
    slots = blk.shape[1]
    nodes = row_blocks * 128
    per_part = row_blocks // PARTS
    chunk_rows = n_harm * ROWS
    me_h = lax.axis_index("harm")
    me_n = lax.axis_index("node")
    pos = me_h * n_node + me_n
    last = n_harm * n_node - 1
    last_n = n_node - 1
    mid = n_harm // 2
    has_prev = pos > 0
    has_next = pos < last
    prev = jnp.maximum(pos - 1, 0)
    following = jnp.minimum(pos + 1, last)
    prev_id = (prev // n_node, prev % n_node)
    next_id = (following // n_node, following % n_node)
    sides = ((has_prev, prev_id, 2), (has_next, next_id, 0))

    at_first = me_n == 0
    at_last = me_n == last_n

    def straight(h, other):
        return jnp.equal(jnp.greater_equal(h, mid), jnp.greater_equal(other, mid))

    direct = [
        [
            (at_first & straight(me_h, t - 1), (t - 1, last_n), t, 2),
            (at_last & straight(me_h, t), (t, 0), t - 1, 0),
        ]
        for t in range(1, n_harm)
    ]
    greeted = [(there, device) for there, device, _ in sides]
    greeted += [(there, device) for pair in direct for there, device, _, _ in pair]
    for h in range(n_harm):
        greeted.append((at_first & (me_h > 0) & straight(h, me_h), (h, last_n)))
        greeted.append((at_last & (me_h < n_harm - 1) & straight(h, me_h), (h, 0)))

    low = me_h < mid
    high = me_h >= mid
    origin = (at_first & high, at_last & low)
    goal = ((mid - 1, last_n), (mid, 0))
    at_goal = ((me_h == mid - 1) & at_last, (me_h == mid) & at_first)
    group = (mid, mid - 1)
    far = (range(mid, n_harm), range(mid))
    start_n = (0, last_n)

    def way_n(p, side, h):
        column = p % 4 if p % 4 < 3 else 1 + h % 2
        return last_n - 2 * column - (1 - side)

    def at_way(p, side):
        return (low if side else high) & (me_n == way_n(p, side, me_h))

    bends = [(p, side) for p in range(PARTS) for side in range(2) if side == 0 or p % 4]
    for p in range(PARTS):
        for side in range(2):
            greeted += [(at_goal[side], (h, way_n(p, side, h))) for h in far[side]]
            greeted.append((at_way(p, side), goal[side]))
            if (p, side) in bends:
                greeted.append((at_way(p, side), (me_h, start_n[side])))
                greeted.append((origin[side], (me_h, way_n(p, side, me_h))))

    adj_loads = [
        pltpu.make_async_copy(
            adj_any.at[pl.ds(c * ROWS, ROWS)], adj.at[pl.ds(c * ROWS, ROWS)], adj_sem.at[c]
        )
        for c in range(n_chunk)
    ]
    loads = [
        pltpu.make_async_copy(there, here, load_sem.at[i])
        for i, (there, here) in enumerate(
            (
                (weight_any, weight),
                (zone_any, zone),
                (fourier_any, fourier),
                (fourier_t_any, fourier_t),
                (capacity_any, capacity),
                (inv_diag_any, inv_diag),
                (cols_any, cols),
                (rad_any, rad),
                (src_any, src),
                (blk_any, blk),
            )
        )
    ]
    for load in adj_loads:
        load.start()

    barrier = pltpu.get_barrier_semaphore()

    def greet(device):
        pl.semaphore_signal(barrier, inc=1, device_id=device, device_id_type=MESH)

    for d in range(1, n_harm):
        greet((lax.rem(me_h + d, n_harm), me_n))
    for there, device in greeted:
        pl.when(there)(functools.partial(greet, device))

    for load in loads:
        load.start()

    tile_rows = n_harm * ROWS

    def spread(c):
        def step(i, carry):
            at = pl.ds(pl.multiple_of(i * (TILES * 128), TILES * 128), TILES * 128)
            x = adj[c * ROWS : (c + 1) * ROWS, :, at]
            x = x.reshape(tile_rows, TILES * 128).astype(jnp.float32)
            for t in range(TILES):
                stage[t * tile_rows : (t + 1) * tile_rows, :] = x[:, t * 128 : (t + 1) * 128]
            for s in range(n_harm):
                for t in range(TILES):
                    rows = stage[pl.ds(t * tile_rows + s, ROWS, stride=n_harm), :]
                    sent[s, c, i * TILES + t] = rows.astype(jnp.bfloat16)
            return carry

        lax.fori_loop(0, row_blocks // TILES, step, 0)

    def of_part(p, start=0):
        return pl.ds(start + p * per_part, per_part)

    def arrive(d, c, p):
        peer = lax.rem(me_h + d, n_harm)
        return pltpu.make_async_remote_copy(
            src_ref=sent.at[peer, c, of_part(p)],
            dst_ref=ext[c].at[me_h, of_part(p, row_blocks)],
            send_sem=in_send.at[d, c, p],
            recv_sem=in_recv.at[d, c, p],
            device_id=(peer, me_n),
            device_id_type=MESH,
        )

    def own(c):
        return pltpu.make_async_copy(
            sent.at[me_h, c], ext[c].at[me_h, pl.ds(row_blocks, row_blocks)], own_in.at[c]
        )

    def halo(piece, c, p, side, mine=False):
        _, device, place = sides[side]
        if mine:
            source = sent.at[me_h, c, of_part(p)]
        else:
            source = ext[c].at[piece, of_part(p, row_blocks)]
        return pltpu.make_async_remote_copy(
            src_ref=source,
            dst_ref=ext[c].at[piece, of_part(p, place * row_blocks)],
            send_sem=halo_send.at[side, piece, c, p],
            recv_sem=halo_recv.at[side, piece, c, p],
            device_id=device,
            device_id_type=MESH,
        )

    def direct_halo(c, p, t, side):
        _, device, s, place = direct[t][side]
        return pltpu.make_async_remote_copy(
            src_ref=sent.at[s, c, of_part(p)],
            dst_ref=ext[c].at[me_h, of_part(p, place * row_blocks)],
            send_sem=direct_send.at[t, c, p],
            recv_sem=halo_recv.at[side, me_h, c, p],
            device_id=device,
            device_id_type=MESH,
        )

    def depart(c, p, side):
        bent = (p, side) in bends
        if bent:
            landing, done = held.at[p, c], bend_recv.at[p, c]
        else:
            landing = ext[c].at[me_h, of_part(p, sides[side][2] * row_blocks)]
            done = halo_recv.at[side, me_h, c, p]
        return pltpu.make_async_remote_copy(
            src_ref=sent.at[group[side], c, of_part(p)],
            dst_ref=landing,
            send_sem=depart_send.at[c, p],
            recv_sem=done,
            device_id=(me_h, way_n(p, side, me_h)) if bent else goal[side],
            device_id_type=MESH,
        )

    def relay_on(c, p, side):
        return pltpu.make_async_remote_copy(
            src_ref=held.at[p, c],
            dst_ref=ext[c].at[me_h, of_part(p, sides[side][2] * row_blocks)],
            send_sem=bend_send.at[p, c],
            recv_sem=halo_recv.at[side, me_h, c, p],
            device_id=goal[side],
            device_id_type=MESH,
        )

    def relay(c):
        for p, side in bends:

            @pl.when(at_way(p, side))
            def _(p=p, side=side):
                depart(c, p, side).wait_recv()
                relay_on(c, p, side).start()

    def piece_of(d):
        return lax.rem(me_h - d + n_harm, n_harm)

    def forwards(d, side):
        piece = piece_of(d)
        if side == 0:
            skip = straight(piece, me_h - 1) | (me_h == mid)
            return has_prev & jnp.logical_not(at_first & skip)
        skip = straight(piece, me_h + 1) | (me_h + 1 == mid)
        return has_next & jnp.logical_not(at_last & skip)

    def start_halo(d, c, p):
        for side in range(2):

            @pl.when(forwards(d, side))
            def _(side=side):
                halo(piece_of(d), c, p, side, mine=d == 0).start()

    order = ORDER if n_harm == 4 else list(range(1, n_harm))
    back_order = BACK if n_harm == 4 else list(range(1, n_harm))

    def send(c):
        for side in range(2):

            @pl.when(origin[side])
            def _(side=side):
                for p in range(PARTS):
                    depart(c, p, side).start()

        if c in MAJOR:
            for d in order:
                for p in range(PARTS):
                    arrive(d, c, p).start()
        for p in range(PARTS):
            if c not in MAJOR:
                for d in order:
                    arrive(d, c, p).start()
            start_halo(0, c, p)
            for t in range(n_harm - 1):
                for side in range(2):

                    @pl.when(direct[t][side][0])
                    def _(t=t, side=side, p=p):
                        direct_halo(c, p, t, side).start()

        own(c).start()

    adj_loads[0].wait()
    spread(0)
    expected = jnp.int32(n_harm - 1)
    for there, _ in greeted:
        expected = expected + jnp.where(there, jnp.int32(1), jnp.int32(0))
    pl.semaphore_wait(barrier, expected)
    send(0)
    for c in range(1, n_chunk):
        adj_loads[c].wait()
        spread(c)
        relay(c - 1)
        send(c)

    half = chunk_rows // 2
    for c in range(n_chunk):
        row = lax.broadcasted_iota(jnp.int32, (chunk_rows, 128), 0)
        k = (row // ROWS) * (n_chunk * ROWS) + c * ROWS + row % ROWS
        half_k = n_harm * n_chunk * ROWS // 2
        rate = jnp.where(k < half_k, k, half_k - k).astype(jnp.float32)
        rate_k[c * chunk_rows : (c + 1) * chunk_rows, :] = rate

    for load in loads:
        load.wait()

    zone_row = lax.broadcasted_iota(jnp.int32, (128, WIDTH), 0)

    def select_step(i, carry):
        at = pl.ds(pl.multiple_of(i * WIDTH, WIDTH), WIDTH)
        hit = zone_row == (zone[:, at] - (pos - 1) * ZONE_DEV)
        w = weight[:, at]
        high = w.astype(jnp.bfloat16).astype(jnp.float32)
        select[0:128, at] = jnp.where(hit, high, 0.0).astype(jnp.bfloat16)
        select[128:256, at] = jnp.where(hit, w - high, 0.0).astype(jnp.bfloat16)
        return carry

    lax.fori_loop(0, nodes // WIDTH, select_step, 0)
    relay(n_chunk - 1)

    def block_of(c, index):
        return jnp.concatenate([ext[c][h, index] for h in range(n_harm)], axis=0)

    def local_part(p):
        def local_step(i, carry):
            at = pl.ds(pl.multiple_of(i * WIDTH, WIDTH), WIDTH)
            first = row_blocks + i * (WIDTH // 128)
            pieces = [
                jnp.concatenate([block_of(c, first + t) for t in range(WIDTH // 128)], axis=1)
                for c in range(n_chunk)
            ]
            field = jnp.concatenate(pieces, axis=0) if n_chunk > 1 else pieces[0]
            samples = jnp.dot(fourier[...], field, preferred_element_type=jnp.float32)
            weighted = (rad[:, at].astype(jnp.float32) * samples).astype(jnp.bfloat16)
            radiative = jnp.dot(fourier_t[...], weighted, preferred_element_type=jnp.float32)
            cap = capacity[:, at]
            for c in range(n_chunk):
                lam = pieces[c].astype(jnp.float32)
                swapped = jnp.concatenate([lam[half:], lam[:half]], axis=0)
                rows = slice(c * chunk_rows, (c + 1) * chunk_rows)
                k = jnp.concatenate([rate_k[rows, :]] * (WIDTH // 128), axis=1)
                rate = k * swapped
                rest = src[:, c, :, at].reshape(chunk_rows, WIDTH) - (cap * rate + radiative[rows])
                src[:, c, :, at] = rest.reshape(n_harm, ROWS, WIDTH)
            return carry

        steps = nodes // PARTS // WIDTH
        lax.fori_loop(p * steps, (p + 1) * steps, local_step, 0)

    def back(d, c, p):
        peer = lax.rem(me_h + d, n_harm)
        return pltpu.make_async_remote_copy(
            src_ref=upd.at[peer, c, of_part(p)],
            dst_ref=ret.at[me_h, c, of_part(p)],
            send_sem=out_send.at[d, c, p],
            recv_sem=out_recv.at[d, c, p],
            device_id=(peer, me_n),
            device_id_type=MESH,
        )

    def own_back(c, p):
        return pltpu.make_async_copy(
            upd.at[me_h, c, of_part(p)], ret.at[me_h, c, of_part(p)], own_out.at[c, p]
        )

    def conduct(c, p):
        def block_step(i, carry):
            b = p * per_part + i
            at = pl.ds(pl.multiple_of(b * 128, 128), 128)
            lam = block_of(c, row_blocks + b)
            taken = [lam]
            for s in range(1, slots):
                col = cols[s, b] - (pos - 1) * row_blocks
                col = jnp.minimum(jnp.maximum(col, 0), 3 * row_blocks - 1)
                taken.append(block_of(c, col))
            conductance = jnp.concatenate([blk[b, s] for s in range(slots)], axis=1)
            conduction = lax.dot_general(
                jnp.concatenate(taken, axis=1),
                conductance,
                NT,
                preferred_element_type=jnp.float32,
            )
            residual = src[:, c, :, at].reshape(chunk_rows, 128) - conduction
            new = lam.astype(jnp.float32) + inv_diag[:, at] * residual
            upd[:, c, b] = new.astype(jnp.bfloat16).reshape(n_harm, ROWS, 128)
            return carry

        lax.fori_loop(0, per_part, block_step, 0, unroll=2)
        for d in back_order:
            back(d, c, p).start()
        own_back(c, p).start()

    def wait_halo(c):
        for side in range(2):

            @pl.when(sides[1 - side][0])
            def _(side=side):
                for p in range(PARTS):
                    for piece in range(n_harm):
                        halo(piece, c, p, side).wait_recv()

    def take(c, p):
        if p == 0:
            own(c).wait()
        for d in range(1, n_harm):
            arrive(d, c, p).wait_recv()
            start_halo(d, c, p)

    final = n_chunk - 1
    for c in range(final):
        for p in range(PARTS):
            take(c, p)
    done = 0
    for p in range(PARTS):
        take(final, p)
        local_part(p)
        if final > 0 and p >= EARLY:
            if done == 0:
                wait_halo(0)
            while done < p - LAG + 1:
                conduct(0, done)
                done += 1
    for c in range(n_chunk):
        if c > 0 or done == 0:
            wait_halo(c)
        for p in range(done if c == 0 else 0, PARTS):
            conduct(c, p)

    part[...] = jnp.zeros_like(part)
    wide = 512 // 128

    def gradient_step(i, carry):
        at = pl.ds(pl.multiple_of(i * 512, 512), 512)
        new = jnp.concatenate(
            [
                upd[:, :, i * wide + t].reshape(n_harm * n_chunk * ROWS, 128)
                for t in range(wide)
            ],
            axis=1,
        )
        both = lax.dot_general(select[:, at], new, NT, preferred_element_type=jnp.float32)
        part[...] += both[0:128] + both[128:256]
        return carry

    lax.fori_loop(0, nodes // 512, gradient_step, 0)

    def hand_over(side):
        _, device, place = sides[side]
        rows = pl.ds(0 if side == 0 else 2 * ZONE_DEV, ZONE_DEV)
        return pltpu.make_async_remote_copy(
            src_ref=part.at[rows, :],
            dst_ref=from_next if side == 0 else from_prev,
            send_sem=part_send.at[side],
            recv_sem=part_recv.at[side],
            device_id=device,
            device_id_type=MESH,
        )

    for side in range(2):

        @pl.when(sides[side][0])
        def _(side=side):
            hand_over(side).start()

    grad[...] = part[ZONE_DEV : 2 * ZONE_DEV, :]

    for side, buffer in ((0, from_next), (1, from_prev)):

        @pl.when(sides[1 - side][0])
        def _(side=side, buffer=buffer):
            hand_over(side).wait_recv()
            grad[...] += buffer[...]

    def gather(c, p):
        def step(i, carry):
            b = p * per_part + i * TILES
            at = pl.ds(pl.multiple_of(b * 128, 128), TILES * 128)
            for s in range(n_harm):
                for t in range(TILES):
                    stage[pl.ds(t * tile_rows + s, ROWS, stride=n_harm), :] = ret[
                        s, c, b + t
                    ].astype(jnp.float32)
            x = jnp.concatenate(
                [stage[t * tile_rows : (t + 1) * tile_rows, :] for t in range(TILES)], axis=1
            )
            x = x.astype(jnp.bfloat16).reshape(ROWS, n_harm, TILES * 128)
            out[c * ROWS : (c + 1) * ROWS, :, at] = x
            return carry

        lax.fori_loop(0, per_part // TILES, step, 0)

    for c in range(n_chunk):
        for p in range(PARTS):
            own_back(c, p).wait()
            for d in range(1, n_harm):
                back(d, c, p).wait_recv()
            gather(c, p)

    for c in range(n_chunk):
        for p in range(PARTS):
            for d in range(1, n_harm):
                arrive(d, c, p).wait_send()
                back(d, c, p).wait_send()
            for side in range(2):
                for t in range(n_harm - 1):

                    @pl.when(direct[t][side][0])
                    def _(t=t, side=side, c=c, p=p):
                        direct_halo(c, p, t, side).wait_send()

                for d in range(n_harm):

                    @pl.when(forwards(d, side))
                    def _(side=side, d=d, c=c, p=p):
                        halo(piece_of(d), c, p, side, mine=d == 0).wait_send()

    for c in range(n_chunk):
        for side in range(2):

            @pl.when(origin[side])
            def _(c=c, side=side):
                for p in range(PARTS):
                    depart(c, p, side).wait_send()

        for p, side in bends:

            @pl.when(at_way(p, side))
            def _(c=c, p=p, side=side):
                relay_on(c, p, side).wait_send()

    for side in range(2):

        @pl.when(sides[side][0])
        def _(side=side):
            hand_over(side).wait_send()


def write_out(updated, gradient, out, grad, sems):
    rows = updated.shape[0] // SLICES
    copies = [pltpu.make_async_copy(gradient, grad, sems.at[SLICES])]
    for i in range(SLICES):
        at = pl.ds(i * rows, rows)
        copies.append(pltpu.make_async_copy(updated.at[at], out.at[at], sems.at[i]))
    for copy in copies:
        copy.start()
    for copy in copies:
        copy.wait()


def body(
    n_harm,
    n_node,
    adjoint,
    source,
    rad_coeff,
    capacity,
    inv_diag,
    blocks,
    block_cols,
    zone_of,
    heater_weight,
):
    rows, _, nodes = adjoint.shape
    n_chunk = rows // ROWS
    harmonics = n_harm * rows
    order = np.arange(harmonics).reshape(n_harm, n_chunk, ROWS).transpose(1, 0, 2).reshape(-1)
    basis = fourier_basis(harmonics)

    row_blocks = nodes // 128
    vmem = pl.BlockSpec(memory_space=pltpu.VMEM)
    hbm = pl.BlockSpec(memory_space=pltpu.HBM)
    piece = (n_harm, n_chunk, ROWS, nodes)
    tiles = (n_harm, n_chunk, row_blocks, ROWS, 128)
    line = (1, nodes)
    dma = pltpu.SemaphoreType.DMA
    updated, gradient = pl.pallas_call(
        functools.partial(kernel, n_harm, n_node, n_chunk),
        out_shape=(
            jax.ShapeDtypeStruct(adjoint.shape, jnp.bfloat16),
            jax.ShapeDtypeStruct((ZONE_DEV, harmonics), jnp.float32),
        ),
        in_specs=[hbm] * 11,
        out_specs=(vmem, vmem),
        scratch_shapes=[pltpu.VMEM((n_harm, 3 * row_blocks, ROWS, 128), jnp.bfloat16)] * n_chunk
        + [
            pltpu.VMEM(adjoint.shape, jnp.bfloat16),
            pltpu.VMEM(piece, jnp.float32),
            pltpu.VMEM(rad_coeff.shape, jnp.bfloat16),
            pltpu.VMEM(blocks.shape, jnp.bfloat16),
            pltpu.VMEM(line, jnp.float32),
            pltpu.VMEM(line, jnp.float32),
            pltpu.VMEM(line, jnp.float32),
            pltpu.VMEM(line, jnp.int32),
            pltpu.SMEM(block_cols.shape[::-1], jnp.int32),
            pltpu.VMEM((harmonics, harmonics), jnp.bfloat16),
            pltpu.VMEM((harmonics, harmonics), jnp.bfloat16),
            pltpu.VMEM((TILES * n_harm * ROWS, 128), jnp.float32),
            pltpu.VMEM(tiles, jnp.bfloat16),
            pltpu.VMEM((harmonics, 128), jnp.float32),
            pltpu.VMEM(tiles, jnp.bfloat16),
            pltpu.VMEM(tiles, jnp.bfloat16),
            pltpu.VMEM((256, nodes), jnp.bfloat16),
            pltpu.VMEM((128, harmonics), jnp.float32),
            pltpu.VMEM((ZONE_DEV, harmonics), jnp.float32),
            pltpu.VMEM((ZONE_DEV, harmonics), jnp.float32),
            dma((10,)),
            dma((n_chunk,)),
            dma((n_chunk,)),
            dma((n_harm, n_chunk, PARTS)),
            dma((n_harm, n_chunk, PARTS)),
            dma((2, n_harm, n_chunk, PARTS)),
            dma((2, n_harm, n_chunk, PARTS)),
            dma((n_harm - 1, n_chunk, PARTS)),
            dma((n_harm, n_chunk, PARTS)),
            dma((n_harm, n_chunk, PARTS)),
            dma((n_chunk, PARTS)),
            dma((2,)),
            dma((2,)),
            pltpu.VMEM((PARTS, n_chunk, row_blocks // PARTS, ROWS, 128), jnp.bfloat16),
            dma((n_chunk, PARTS)),
            dma((PARTS, n_chunk)),
            dma((PARTS, n_chunk)),
        ],
        compiler_params=pltpu.CompilerParams(
            collective_id=0, has_side_effects=True, vmem_limit_bytes=48 * 2**20
        ),
    )(
        *(
            pltpu.with_memory_space_constraint(x, pltpu.HBM)
            for x in (
                adjoint,
                source.reshape(piece),
                rad_coeff,
                blocks,
                capacity[None, :],
                inv_diag[None, :],
                heater_weight[None, :],
                zone_of[None, :],
                block_cols.T,
                jnp.asarray(basis[:, order]),
                jnp.asarray(basis.T[order]),
            )
        )
    )
    return pl.pallas_call(
        write_out,
        out_shape=(
            jax.ShapeDtypeStruct(updated.shape, updated.dtype),
            jax.ShapeDtypeStruct(gradient.shape, gradient.dtype),
        ),
        in_specs=[vmem, vmem],
        out_specs=(hbm, hbm),
        scratch_shapes=[dma((SLICES + 1,))],
    )(
        pltpu.with_memory_space_constraint(updated, pltpu.VMEM),
        pltpu.with_memory_space_constraint(gradient, pltpu.VMEM),
    )


def solution(mesh):
    in_specs = (
        P("harm", None, "node"),
        P(None, ("harm", "node")),
        P(None, ("harm", "node")),
        P(("harm", "node")),
        P(("harm", "node")),
        P(("harm", "node"), None, None, None),
        P(("harm", "node"), None),
        P(("harm", "node")),
        P(("harm", "node")),
    )
    out_specs = (P("harm", None, "node"), P(("harm", "node"), None))
    step = functools.partial(body, mesh.shape["harm"], mesh.shape["node"])
    return jax.shard_map(step, mesh=mesh, in_specs=in_specs, out_specs=out_specs, check_vma=False)
```

```python
import functools
import math

import jax
import jax.numpy as jnp
import numpy as np
from jax import lax
from jax.experimental import pallas as pl
from jax.experimental.pallas import tpu as pltpu
from jax.sharding import PartitionSpec as P

ZONE_DEV = 40
ROWS = 16
PARTS = 4
LAST = (0, 0)
HOLD = 1
PREF = 1
DEFER = 1
DYN = 1
ORDER = [3, 2, 1]
SLICES = 4
EARLY = 0
LAG = 0
WIDTH = 256
TILES = 8
MESH = pl.DeviceIdType.MESH
NT = (((1,), (1,)), ((), ()))


def fourier_basis(count):
    sample_index = np.arange(count, dtype=np.float32)[:, None]
    column_index = np.arange(count)[None, :]
    half_count = count // 2
    frequency = np.where(
        column_index <= half_count, column_index, column_index - half_count
    ).astype(np.float32)
    angle = np.float32(2.0 * math.pi) * frequency * sample_index / np.float32(count)
    values_table = np.where(column_index <= half_count, np.cos(angle), np.sin(angle))
    scaling = np.where(
        (column_index == 0) | (column_index == half_count),
        math.sqrt(1.0 / count),
        math.sqrt(2.0 / count),
    ).astype(np.float32)
    return (values_table * scaling).astype(jnp.bfloat16)


def kernel(n_harm, n_node, n_chunk, *refs):
    (
        adj_any,
        src_any,
        rad_any,
        blk_any,
        capacity_any,
        inv_diag_any,
        weight_any,
        zone_any,
        cols_any,
        fourier_any,
        fourier_t_any,
        out,
        grad,
    ) = refs[:13]
    ext = refs[13 : 13 + n_chunk]
    (
        adj,
        src,
        rad,
        blk,
        capacity,
        inv_diag,
        weight,
        zone,
        cols,
        fourier,
        fourier_t,
        stage,
        sent,
        rate_k,
        upd,
        ret,
        select,
        part,
        from_prev,
        from_next,
        load_sem,
        adj_sem,
        own_in,
        in_send,
        in_recv,
        halo_send,
        halo_recv,
        direct_send,
        out_send,
        out_recv,
        own_out,
        part_send,
        part_recv,
        held,
        depart_send,
        bend_send,
        bend_recv,
    ) = refs[13 + n_chunk :]
    row_blocks = blk.shape[0]
    slots = blk.shape[1]
    nodes = row_blocks * 128
    per_part = row_blocks // PARTS
    chunk_rows = n_harm * ROWS
    me_h = lax.axis_index("harm")
    me_n = lax.axis_index("node")
    pos = me_h * n_node + me_n
    last = n_harm * n_node - 1
    last_n = n_node - 1
    mid = n_harm // 2
    has_prev = pos > 0
    has_next = pos < last
    prev = jnp.maximum(pos - 1, 0)
    following = jnp.minimum(pos + 1, last)
    prev_id = (prev // n_node, prev % n_node)
    next_id = (following // n_node, following % n_node)
    sides = ((has_prev, prev_id, 2), (has_next, next_id, 0))

    at_first = me_n == 0
    at_last = me_n == last_n

    def straight(h, other):
        return jnp.equal(jnp.greater_equal(h, mid), jnp.greater_equal(other, mid))

    direct = [
        [
            (at_first & straight(me_h, t - 1), (t - 1, last_n), t, 2),
            (at_last & straight(me_h, t), (t, 0), t - 1, 0),
        ]
        for t in range(1, n_harm)
    ]
    greeted = [(there, device) for there, device, _ in sides]
    greeted += [(there, device) for pair in direct for there, device, _, _ in pair]
    for h in range(n_harm):
        greeted.append((at_first & (me_h > 0) & straight(h, me_h), (h, last_n)))
        greeted.append((at_last & (me_h < n_harm - 1) & straight(h, me_h), (h, 0)))

    low = me_h < mid
    high = me_h >= mid
    origin = (at_first & high, at_last & low)
    goal = ((mid - 1, last_n), (mid, 0))
    at_goal = ((me_h == mid - 1) & at_last, (me_h == mid) & at_first)
    group = (mid, mid - 1)
    far = (range(mid, n_harm), range(mid))
    start_n = (0, last_n)

    def way_n(p, side, h):
        column = p % 4 if p % 4 < 3 else 1 + h % 2
        return last_n - 2 * column - (1 - side)

    def at_way(p, side):
        return (low if side else high) & (me_n == way_n(p, side, me_h))

    bends = [(p, side) for p in range(PARTS) for side in range(2) if side == 0 or p % 4]
    for p in range(PARTS):
        for side in range(2):
            greeted += [(at_goal[side], (h, way_n(p, side, h))) for h in far[side]]
            greeted.append((at_way(p, side), goal[side]))
            if (p, side) in bends:
                greeted.append((at_way(p, side), (me_h, start_n[side])))
                greeted.append((origin[side], (me_h, way_n(p, side, me_h))))

    adj_loads = [
        pltpu.make_async_copy(
            adj_any.at[pl.ds(c * ROWS, ROWS)], adj.at[pl.ds(c * ROWS, ROWS)], adj_sem.at[c]
        )
        for c in range(n_chunk)
    ]
    loads = [
        pltpu.make_async_copy(there, here, load_sem.at[i])
        for i, (there, here) in enumerate(
            (
                (weight_any, weight),
                (zone_any, zone),
                (fourier_any, fourier),
                (fourier_t_any, fourier_t),
                (capacity_any, capacity),
                (inv_diag_any, inv_diag),
                (cols_any, cols),
                (rad_any, rad),
                (src_any, src),
                (blk_any, blk),
            )
        )
    ]
    for load in adj_loads:
        load.start()

    barrier = pltpu.get_barrier_semaphore()

    def greet(device):
        pl.semaphore_signal(barrier, inc=1, device_id=device, device_id_type=MESH)

    for d in range(1, n_harm):
        greet((lax.rem(me_h + d, n_harm), me_n))
    for there, device in greeted:
        pl.when(there)(functools.partial(greet, device))

    for load in loads:
        load.start()

    tile_rows = n_harm * ROWS

    def spread(c):
        def step(i, carry):
            at = pl.ds(pl.multiple_of(i * (TILES * 128), TILES * 128), TILES * 128)
            x = adj[c * ROWS : (c + 1) * ROWS, :, at]
            x = x.reshape(tile_rows, TILES * 128).astype(jnp.float32)
            for t in range(TILES):
                stage[t * tile_rows : (t + 1) * tile_rows, :] = x[:, t * 128 : (t + 1) * 128]
            for s in range(n_harm):
                for t in range(TILES):
                    rows = stage[pl.ds(t * tile_rows + s, ROWS, stride=n_harm), :]
                    sent[s, c, i * TILES + t] = rows.astype(jnp.bfloat16)
            return carry

        lax.fori_loop(0, row_blocks // TILES, step, 0)

    def of_part(p, start=0):
        return pl.ds(start + p * per_part, per_part)

    def arrive(d, c, p):
        peer = lax.rem(me_h + d, n_harm)
        return pltpu.make_async_remote_copy(
            src_ref=sent.at[peer, c, of_part(p)],
            dst_ref=ext[c].at[me_h, of_part(p, row_blocks)],
            send_sem=in_send.at[d, c, p],
            recv_sem=in_recv.at[d, c, p],
            device_id=(peer, me_n),
            device_id_type=MESH,
        )

    def own(c):
        return pltpu.make_async_copy(
            sent.at[me_h, c], ext[c].at[me_h, pl.ds(row_blocks, row_blocks)], own_in.at[c]
        )

    def halo(piece, c, p, side, mine=False):
        _, device, place = sides[side]
        if mine:
            source = sent.at[me_h, c, of_part(p)]
        else:
            source = ext[c].at[piece, of_part(p, row_blocks)]
        return pltpu.make_async_remote_copy(
            src_ref=source,
            dst_ref=ext[c].at[piece, of_part(p, place * row_blocks)],
            send_sem=halo_send.at[side, piece, c, p],
            recv_sem=halo_recv.at[side, piece, c, p],
            device_id=device,
            device_id_type=MESH,
        )

    def direct_halo(c, p, t, side):
        _, device, s, place = direct[t][side]
        return pltpu.make_async_remote_copy(
            src_ref=sent.at[s, c, of_part(p)],
            dst_ref=ext[c].at[me_h, of_part(p, place * row_blocks)],
            send_sem=direct_send.at[t, c, p],
            recv_sem=halo_recv.at[side, me_h, c, p],
            device_id=device,
            device_id_type=MESH,
        )

    def depart(c, p, side):
        bent = (p, side) in bends
        if bent:
            landing, done = held.at[p, c], bend_recv.at[p, c]
        else:
            landing = ext[c].at[me_h, of_part(p, sides[side][2] * row_blocks)]
            done = halo_recv.at[side, me_h, c, p]
        return pltpu.make_async_remote_copy(
            src_ref=sent.at[group[side], c, of_part(p)],
            dst_ref=landing,
            send_sem=depart_send.at[c, p],
            recv_sem=done,
            device_id=(me_h, way_n(p, side, me_h)) if bent else goal[side],
            device_id_type=MESH,
        )

    def relay_on(c, p, side):
        return pltpu.make_async_remote_copy(
            src_ref=held.at[p, c],
            dst_ref=ext[c].at[me_h, of_part(p, sides[side][2] * row_blocks)],
            send_sem=bend_send.at[p, c],
            recv_sem=halo_recv.at[side, me_h, c, p],
            device_id=goal[side],
            device_id_type=MESH,
        )

    def relay(c):
        for p, side in bends:

            @pl.when(at_way(p, side))
            def _(p=p, side=side):
                depart(c, p, side).wait_recv()
                relay_on(c, p, side).start()

    def piece_of(d):
        return lax.rem(me_h - d + n_harm, n_harm)

    def forwards(d, side):
        piece = piece_of(d)
        if side == 0:
            skip = straight(piece, me_h - 1) | (me_h == mid)
            return has_prev & jnp.logical_not(at_first & skip)
        skip = straight(piece, me_h + 1) | (me_h + 1 == mid)
        return has_next & jnp.logical_not(at_last & skip)

    def start_halo(d, c, p):
        for side in range(2):

            @pl.when(forwards(d, side))
            def _(side=side):
                halo(piece_of(d), c, p, side, mine=d == 0).start()

    order = ORDER if n_harm == 4 else list(range(1, n_harm))
    if DYN and n_harm == 4:
        order = [jnp.int32(2), jnp.where(low, 3, 1), jnp.where(low, 1, 3)]
    back_order = order
    if PREF and n_harm == 4:
        odd = me_h % 2
        back_order = [2 - odd, 3 - odd, 1 + 2 * odd]
        if PREF == 2:
            back_order = [2 - odd, 1 + 2 * odd, 3 - odd]

    def send(c):
        for side in range(2):

            @pl.when(origin[side])
            def _(side=side):
                for p in range(PARTS):
                    depart(c, p, side).start()

        if LAST[c] == 3:
            for p in range(PARTS):
                arrive(order[-1], c, p).start()
        for p in range(PARTS):
            for d in order if LAST[c] < 2 else order[:-1]:
                arrive(d, c, p).start()
        if LAST[c] == 2:
            for p in range(PARTS):
                arrive(order[-1], c, p).start()
        for p in range(PARTS):
            start_halo(0, c, p)
            for t in range(n_harm - 1):
                for side in range(2):

                    @pl.when(direct[t][side][0])
                    def _(t=t, side=side, p=p):
                        direct_halo(c, p, t, side).start()

        own(c).start()

    adj_loads[0].wait()
    spread(0)
    expected = jnp.int32(n_harm - 1)
    for there, _ in greeted:
        expected = expected + jnp.where(there, jnp.int32(1), jnp.int32(0))
    pl.semaphore_wait(barrier, expected)
    send(0)
    for c in range(1, n_chunk):
        adj_loads[c].wait()
        spread(c)
        relay(c - 1)
        send(c)

    half = chunk_rows // 2
    for c in range(n_chunk):
        row = lax.broadcasted_iota(jnp.int32, (chunk_rows, 128), 0)
        k = (row // ROWS) * (n_chunk * ROWS) + c * ROWS + row % ROWS
        half_k = n_harm * n_chunk * ROWS // 2
        rate = jnp.where(k < half_k, k, half_k - k).astype(jnp.float32)
        rate_k[c * chunk_rows : (c + 1) * chunk_rows, :] = rate

    for load in loads:
        load.wait()

    zone_row = lax.broadcasted_iota(jnp.int32, (128, WIDTH), 0)

    def select_step(i, carry):
        at = pl.ds(pl.multiple_of(i * WIDTH, WIDTH), WIDTH)
        hit = zone_row == (zone[:, at] - (pos - 1) * ZONE_DEV)
        w = weight[:, at]
        high = w.astype(jnp.bfloat16).astype(jnp.float32)
        select[0:128, at] = jnp.where(hit, high, 0.0).astype(jnp.bfloat16)
        select[128:256, at] = jnp.where(hit, w - high, 0.0).astype(jnp.bfloat16)
        return carry

    lax.fori_loop(0, nodes // WIDTH, select_step, 0)
    relay(n_chunk - 1)

    def block_of(c, index):
        return jnp.concatenate([ext[c][h, index] for h in range(n_harm)], axis=0)

    def local_part(p):
        def local_step(i, carry):
            at = pl.ds(pl.multiple_of(i * WIDTH, WIDTH), WIDTH)
            first = row_blocks + i * (WIDTH // 128)
            pieces = [
                jnp.concatenate([block_of(c, first + t) for t in range(WIDTH // 128)], axis=1)
                for c in range(n_chunk)
            ]
            field = jnp.concatenate(pieces, axis=0) if n_chunk > 1 else pieces[0]
            samples = jnp.dot(fourier[...], field, preferred_element_type=jnp.float32)
            weighted = (rad[:, at].astype(jnp.float32) * samples).astype(jnp.bfloat16)
            radiative = jnp.dot(fourier_t[...], weighted, preferred_element_type=jnp.float32)
            cap = capacity[:, at]
            for c in range(n_chunk):
                lam = pieces[c].astype(jnp.float32)
                swapped = jnp.concatenate([lam[half:], lam[:half]], axis=0)
                rows = slice(c * chunk_rows, (c + 1) * chunk_rows)
                k = jnp.concatenate([rate_k[rows, :]] * (WIDTH // 128), axis=1)
                rate = k * swapped
                rest = src[:, c, :, at].reshape(chunk_rows, WIDTH) - (cap * rate + radiative[rows])
                src[:, c, :, at] = rest.reshape(n_harm, ROWS, WIDTH)
            return carry

        steps = nodes // PARTS // WIDTH
        lax.fori_loop(p * steps, (p + 1) * steps, local_step, 0)

    def back(d, c, p):
        peer = lax.rem(me_h + d, n_harm)
        return pltpu.make_async_remote_copy(
            src_ref=upd.at[peer, c, of_part(p)],
            dst_ref=ret.at[me_h, c, of_part(p)],
            send_sem=out_send.at[d, c, p],
            recv_sem=out_recv.at[d, c, p],
            device_id=(peer, me_n),
            device_id_type=MESH,
        )

    def own_back(c, p):
        return pltpu.make_async_copy(
            upd.at[me_h, c, of_part(p)], ret.at[me_h, c, of_part(p)], own_out.at[c, p]
        )

    def conduct(c, p):
        def block_step(i, carry):
            b = p * per_part + i
            at = pl.ds(pl.multiple_of(b * 128, 128), 128)
            lam = block_of(c, row_blocks + b)
            taken = [lam]
            for s in range(1, slots):
                col = cols[s, b] - (pos - 1) * row_blocks
                col = jnp.minimum(jnp.maximum(col, 0), 3 * row_blocks - 1)
                taken.append(block_of(c, col))
            conductance = jnp.concatenate([blk[b, s] for s in range(slots)], axis=1)
            conduction = lax.dot_general(
                jnp.concatenate(taken, axis=1),
                conductance,
                NT,
                preferred_element_type=jnp.float32,
            )
            residual = src[:, c, :, at].reshape(chunk_rows, 128) - conduction
            new = lam.astype(jnp.float32) + inv_diag[:, at] * residual
            upd[:, c, b] = new.astype(jnp.bfloat16).reshape(n_harm, ROWS, 128)
            return carry

        lax.fori_loop(0, per_part, block_step, 0, unroll=2)
        if c < n_chunk - 1 or p < PARTS - HOLD:
            give(c, p)

    def give(c, p):
        own_back(c, p).start()
        back(back_order[0], c, p).start()
        if c < n_chunk - 1 or DEFER == 0:
            for d in back_order[1:]:
                back(d, c, p).start()
        else:
            flush = range(p - DEFER, PARTS if p == PARTS - 1 else p - DEFER + 1)
            for late in flush:
                if late >= 0:
                    for d in back_order[1:]:
                        back(d, c, late).start()

    def wait_halo(c):
        for side in range(2):

            @pl.when(sides[1 - side][0])
            def _(side=side):
                for p in range(PARTS):
                    for piece in range(n_harm):
                        halo(piece, c, p, side).wait_recv()

    def take(c, p):
        if p == 0:
            own(c).wait()
        for d in range(1, n_harm):
            arrive(d, c, p).wait_recv()
            start_halo(d, c, p)

    final = n_chunk - 1
    for c in range(final):
        for p in range(PARTS):
            take(c, p)
    done = 0
    for p in range(PARTS):
        take(final, p)
        local_part(p)
        if final > 0 and p >= EARLY:
            if done == 0:
                wait_halo(0)
            while done < p - LAG + 1:
                conduct(0, done)
                done += 1
    for c in range(n_chunk):
        if c > 0 or done == 0:
            wait_halo(c)
        for p in range(done if c == 0 else 0, PARTS):
            conduct(c, p)

    part[...] = jnp.zeros_like(part)
    wide = 512 // 128

    def gradient_step(i, carry):
        at = pl.ds(pl.multiple_of(i * 512, 512), 512)
        new = jnp.concatenate(
            [
                upd[:, :, i * wide + t].reshape(n_harm * n_chunk * ROWS, 128)
                for t in range(wide)
            ],
            axis=1,
        )
        both = lax.dot_general(select[:, at], new, NT, preferred_element_type=jnp.float32)
        part[...] += both[0:128] + both[128:256]
        return carry

    lax.fori_loop(0, nodes // 512, gradient_step, 0)

    def hand_over(side):
        _, device, place = sides[side]
        rows = pl.ds(0 if side == 0 else 2 * ZONE_DEV, ZONE_DEV)
        return pltpu.make_async_remote_copy(
            src_ref=part.at[rows, :],
            dst_ref=from_next if side == 0 else from_prev,
            send_sem=part_send.at[side],
            recv_sem=part_recv.at[side],
            device_id=device,
            device_id_type=MESH,
        )

    for side in range(2):

        @pl.when(sides[side][0])
        def _(side=side):
            hand_over(side).start()

    for p in range(PARTS - HOLD, PARTS):
        give(n_chunk - 1, p)

    grad[...] = part[ZONE_DEV : 2 * ZONE_DEV, :]

    def join():
        for side, buffer in ((0, from_next), (1, from_prev)):

            @pl.when(sides[1 - side][0])
            def _(side=side, buffer=buffer):
                hand_over(side).wait_recv()
                grad[...] += buffer[...]

    def gather(c, p):
        def step(i, carry):
            b = p * per_part + i * TILES
            at = pl.ds(pl.multiple_of(b * 128, 128), TILES * 128)
            for s in range(n_harm):
                for t in range(TILES):
                    stage[pl.ds(t * tile_rows + s, ROWS, stride=n_harm), :] = ret[
                        s, c, b + t
                    ].astype(jnp.float32)
            x = jnp.concatenate(
                [stage[t * tile_rows : (t + 1) * tile_rows, :] for t in range(TILES)], axis=1
            )
            x = x.astype(jnp.bfloat16).reshape(ROWS, n_harm, TILES * 128)
            out[c * ROWS : (c + 1) * ROWS, :, at] = x
            return carry

        lax.fori_loop(0, per_part // TILES, step, 0)

    for c in range(n_chunk):
        for p in range(PARTS):
            own_back(c, p).wait()
            for d in range(1, n_harm):
                back(d, c, p).wait_recv()
            gather(c, p)
            if c == n_chunk - 1 and p == PARTS - 2:
                join()

    for c in range(n_chunk):
        for p in range(PARTS):
            for d in range(1, n_harm):
                arrive(d, c, p).wait_send()
                back(d, c, p).wait_send()
            for side in range(2):
                for t in range(n_harm - 1):

                    @pl.when(direct[t][side][0])
                    def _(t=t, side=side, c=c, p=p):
                        direct_halo(c, p, t, side).wait_send()

                for d in range(n_harm):

                    @pl.when(forwards(d, side))
                    def _(side=side, d=d, c=c, p=p):
                        halo(piece_of(d), c, p, side, mine=d == 0).wait_send()

    for c in range(n_chunk):
        for side in range(2):

            @pl.when(origin[side])
            def _(c=c, side=side):
                for p in range(PARTS):
                    depart(c, p, side).wait_send()

        for p, side in bends:

            @pl.when(at_way(p, side))
            def _(c=c, p=p, side=side):
                relay_on(c, p, side).wait_send()

    for side in range(2):

        @pl.when(sides[side][0])
        def _(side=side):
            hand_over(side).wait_send()


def write_out(updated, gradient, out, grad, sems):
    rows = updated.shape[0] // SLICES
    copies = [pltpu.make_async_copy(gradient, grad, sems.at[SLICES])]
    for i in range(SLICES):
        at = pl.ds(i * rows, rows)
        copies.append(pltpu.make_async_copy(updated.at[at], out.at[at], sems.at[i]))
    for copy in copies:
        copy.start()
    for copy in copies:
        copy.wait()


def body(
    n_harm,
    n_node,
    adjoint,
    source,
    rad_coeff,
    capacity,
    inv_diag,
    blocks,
    block_cols,
    zone_of,
    heater_weight,
):
    rows, _, nodes = adjoint.shape
    n_chunk = rows // ROWS
    harmonics = n_harm * rows
    order = np.arange(harmonics).reshape(n_harm, n_chunk, ROWS).transpose(1, 0, 2).reshape(-1)
    basis = fourier_basis(harmonics)

    row_blocks = nodes // 128
    vmem = pl.BlockSpec(memory_space=pltpu.VMEM)
    hbm = pl.BlockSpec(memory_space=pltpu.HBM)
    piece = (n_harm, n_chunk, ROWS, nodes)
    tiles = (n_harm, n_chunk, row_blocks, ROWS, 128)
    line = (1, nodes)
    dma = pltpu.SemaphoreType.DMA
    updated, gradient = pl.pallas_call(
        functools.partial(kernel, n_harm, n_node, n_chunk),
        out_shape=(
            jax.ShapeDtypeStruct(adjoint.shape, jnp.bfloat16),
            jax.ShapeDtypeStruct((ZONE_DEV, harmonics), jnp.float32),
        ),
        in_specs=[hbm] * 11,
        out_specs=(vmem, vmem),
        scratch_shapes=[pltpu.VMEM((n_harm, 3 * row_blocks, ROWS, 128), jnp.bfloat16)] * n_chunk
        + [
            pltpu.VMEM(adjoint.shape, jnp.bfloat16),
            pltpu.VMEM(piece, jnp.float32),
            pltpu.VMEM(rad_coeff.shape, jnp.bfloat16),
            pltpu.VMEM(blocks.shape, jnp.bfloat16),
            pltpu.VMEM(line, jnp.float32),
            pltpu.VMEM(line, jnp.float32),
            pltpu.VMEM(line, jnp.float32),
            pltpu.VMEM(line, jnp.int32),
            pltpu.SMEM(block_cols.shape[::-1], jnp.int32),
            pltpu.VMEM((harmonics, harmonics), jnp.bfloat16),
            pltpu.VMEM((harmonics, harmonics), jnp.bfloat16),
            pltpu.VMEM((TILES * n_harm * ROWS, 128), jnp.float32),
            pltpu.VMEM(tiles, jnp.bfloat16),
            pltpu.VMEM((harmonics, 128), jnp.float32),
            pltpu.VMEM(tiles, jnp.bfloat16),
            pltpu.VMEM(tiles, jnp.bfloat16),
            pltpu.VMEM((256, nodes), jnp.bfloat16),
            pltpu.VMEM((128, harmonics), jnp.float32),
            pltpu.VMEM((ZONE_DEV, harmonics), jnp.float32),
            pltpu.VMEM((ZONE_DEV, harmonics), jnp.float32),
            dma((10,)),
            dma((n_chunk,)),
            dma((n_chunk,)),
            dma((n_harm, n_chunk, PARTS)),
            dma((n_harm, n_chunk, PARTS)),
            dma((2, n_harm, n_chunk, PARTS)),
            dma((2, n_harm, n_chunk, PARTS)),
            dma((n_harm - 1, n_chunk, PARTS)),
            dma((n_harm, n_chunk, PARTS)),
            dma((n_harm, n_chunk, PARTS)),
            dma((n_chunk, PARTS)),
            dma((2,)),
            dma((2,)),
            pltpu.VMEM((PARTS, n_chunk, row_blocks // PARTS, ROWS, 128), jnp.bfloat16),
            dma((n_chunk, PARTS)),
            dma((PARTS, n_chunk)),
            dma((PARTS, n_chunk)),
        ],
        compiler_params=pltpu.CompilerParams(
            collective_id=0, has_side_effects=True, vmem_limit_bytes=48 * 2**20
        ),
    )(
        *(
            pltpu.with_memory_space_constraint(x, pltpu.HBM)
            for x in (
                adjoint,
                source.reshape(piece),
                rad_coeff,
                blocks,
                capacity[None, :],
                inv_diag[None, :],
                heater_weight[None, :],
                zone_of[None, :],
                block_cols.T,
                jnp.asarray(basis[:, order]),
                jnp.asarray(basis.T[order]),
            )
        )
    )
    return pl.pallas_call(
        write_out,
        out_shape=(
            jax.ShapeDtypeStruct(updated.shape, updated.dtype),
            jax.ShapeDtypeStruct(gradient.shape, gradient.dtype),
        ),
        in_specs=[vmem, vmem],
        out_specs=(hbm, hbm),
        scratch_shapes=[dma((SLICES + 1,))],
    )(
        pltpu.with_memory_space_constraint(updated, pltpu.VMEM),
        pltpu.with_memory_space_constraint(gradient, pltpu.VMEM),
    )


def solution(mesh):
    in_specs = (
        P("harm", None, "node"),
        P(None, ("harm", "node")),
        P(None, ("harm", "node")),
        P(("harm", "node")),
        P(("harm", "node")),
        P(("harm", "node"), None, None, None),
        P(("harm", "node"), None),
        P(("harm", "node")),
        P(("harm", "node")),
    )
    out_specs = (P("harm", None, "node"), P(("harm", "node"), None))
    step = functools.partial(body, mesh.shape["harm"], mesh.shape["node"])
    return jax.shard_map(step, mesh=mesh, in_specs=in_specs, out_specs=out_specs, check_vma=False)
```

```python
import functools
import math

import jax
import jax.numpy as jnp
import numpy as np
from jax import lax
from jax.experimental import pallas as pl
from jax.experimental.pallas import tpu as pltpu
from jax.sharding import PartitionSpec as P

ZONE_DEV = 40
ROWS = 16
PARTS = 4
LAST = (3, 3)
HOLD = 1
PREF = 1
DEFER = 2
DYN = 1
ORDER = [3, 2, 1]
SLICES = 4
EARLY = 0
LAG = 0
WIDTH = 256
TILES = 8
MESH = pl.DeviceIdType.MESH
NT = (((1,), (1,)), ((), ()))


def fourier_basis(count):
    sample_index = np.arange(count, dtype=np.float32)[:, None]
    column_index = np.arange(count)[None, :]
    half_count = count // 2
    frequency = np.where(
        column_index <= half_count, column_index, column_index - half_count
    ).astype(np.float32)
    angle = np.float32(2.0 * math.pi) * frequency * sample_index / np.float32(count)
    values_table = np.where(column_index <= half_count, np.cos(angle), np.sin(angle))
    scaling = np.where(
        (column_index == 0) | (column_index == half_count),
        math.sqrt(1.0 / count),
        math.sqrt(2.0 / count),
    ).astype(np.float32)
    return (values_table * scaling).astype(jnp.bfloat16)


def kernel(n_harm, n_node, n_chunk, *refs):
    (
        adj_any,
        src_any,
        rad_any,
        blk_any,
        capacity_any,
        inv_diag_any,
        weight_any,
        zone_any,
        cols_any,
        fourier_any,
        fourier_t_any,
        out,
        grad,
    ) = refs[:13]
    ext = refs[13 : 13 + n_chunk]
    (
        adj,
        src,
        rad,
        blk,
        capacity,
        inv_diag,
        weight,
        zone,
        cols,
        fourier,
        fourier_t,
        stage,
        sent,
        rate_k,
        upd,
        ret,
        select,
        part,
        from_prev,
        from_next,
        load_sem,
        adj_sem,
        own_in,
        in_send,
        in_recv,
        halo_send,
        halo_recv,
        direct_send,
        out_send,
        out_recv,
        own_out,
        part_send,
        part_recv,
        held,
        depart_send,
        bend_send,
        bend_recv,
    ) = refs[13 + n_chunk :]
    row_blocks = blk.shape[0]
    slots = blk.shape[1]
    nodes = row_blocks * 128
    per_part = row_blocks // PARTS
    chunk_rows = n_harm * ROWS
    me_h = lax.axis_index("harm")
    me_n = lax.axis_index("node")
    pos = me_h * n_node + me_n
    last = n_harm * n_node - 1
    last_n = n_node - 1
    mid = n_harm // 2
    has_prev = pos > 0
    has_next = pos < last
    prev = jnp.maximum(pos - 1, 0)
    following = jnp.minimum(pos + 1, last)
    prev_id = (prev // n_node, prev % n_node)
    next_id = (following // n_node, following % n_node)
    sides = ((has_prev, prev_id, 2), (has_next, next_id, 0))

    at_first = me_n == 0
    at_last = me_n == last_n

    def straight(h, other):
        return jnp.equal(jnp.greater_equal(h, mid), jnp.greater_equal(other, mid))

    direct = [
        [
            (at_first & straight(me_h, t - 1), (t - 1, last_n), t, 2),
            (at_last & straight(me_h, t), (t, 0), t - 1, 0),
        ]
        for t in range(1, n_harm)
    ]
    greeted = [(there, device) for there, device, _ in sides]
    greeted += [(there, device) for pair in direct for there, device, _, _ in pair]
    for h in range(n_harm):
        greeted.append((at_first & (me_h > 0) & straight(h, me_h), (h, last_n)))
        greeted.append((at_last & (me_h < n_harm - 1) & straight(h, me_h), (h, 0)))

    low = me_h < mid
    high = me_h >= mid
    origin = (at_first & high, at_last & low)
    goal = ((mid - 1, last_n), (mid, 0))
    at_goal = ((me_h == mid - 1) & at_last, (me_h == mid) & at_first)
    group = (mid, mid - 1)
    far = (range(mid, n_harm), range(mid))
    start_n = (0, last_n)

    def way_n(p, side, h):
        column = p % 4 if p % 4 < 3 else 1 + h % 2
        return last_n - 2 * column - (1 - side)

    def at_way(p, side):
        return (low if side else high) & (me_n == way_n(p, side, me_h))

    bends = [(p, side) for p in range(PARTS) for side in range(2) if side == 0 or p % 4]
    for p in range(PARTS):
        for side in range(2):
            greeted += [(at_goal[side], (h, way_n(p, side, h))) for h in far[side]]
            greeted.append((at_way(p, side), goal[side]))
            if (p, side) in bends:
                greeted.append((at_way(p, side), (me_h, start_n[side])))
                greeted.append((origin[side], (me_h, way_n(p, side, me_h))))

    adj_loads = [
        pltpu.make_async_copy(
            adj_any.at[pl.ds(c * ROWS, ROWS)], adj.at[pl.ds(c * ROWS, ROWS)], adj_sem.at[c]
        )
        for c in range(n_chunk)
    ]
    loads = [
        pltpu.make_async_copy(there, here, load_sem.at[i])
        for i, (there, here) in enumerate(
            (
                (weight_any, weight),
                (zone_any, zone),
                (fourier_any, fourier),
                (fourier_t_any, fourier_t),
                (capacity_any, capacity),
                (inv_diag_any, inv_diag),
                (cols_any, cols),
                (rad_any, rad),
                (src_any, src),
                (blk_any, blk),
            )
        )
    ]
    for load in adj_loads:
        load.start()

    barrier = pltpu.get_barrier_semaphore()

    def greet(device):
        pl.semaphore_signal(barrier, inc=1, device_id=device, device_id_type=MESH)

    for d in range(1, n_harm):
        greet((lax.rem(me_h + d, n_harm), me_n))
    for there, device in greeted:
        pl.when(there)(functools.partial(greet, device))

    for load in loads:
        load.start()

    tile_rows = n_harm * ROWS

    def spread(c):
        def step(i, carry):
            at = pl.ds(pl.multiple_of(i * (TILES * 128), TILES * 128), TILES * 128)
            x = adj[c * ROWS : (c + 1) * ROWS, :, at]
            x = x.reshape(tile_rows, TILES * 128).astype(jnp.float32)
            for t in range(TILES):
                stage[t * tile_rows : (t + 1) * tile_rows, :] = x[:, t * 128 : (t + 1) * 128]
            for s in range(n_harm):
                for t in range(TILES):
                    rows = stage[pl.ds(t * tile_rows + s, ROWS, stride=n_harm), :]
                    sent[s, c, i * TILES + t] = rows.astype(jnp.bfloat16)
            return carry

        lax.fori_loop(0, row_blocks // TILES, step, 0)

    def of_part(p, start=0):
        return pl.ds(start + p * per_part, per_part)

    def arrive(d, c, p):
        peer = lax.rem(me_h + d, n_harm)
        return pltpu.make_async_remote_copy(
            src_ref=sent.at[peer, c, of_part(p)],
            dst_ref=ext[c].at[me_h, of_part(p, row_blocks)],
            send_sem=in_send.at[d, c, p],
            recv_sem=in_recv.at[d, c, p],
            device_id=(peer, me_n),
            device_id_type=MESH,
        )

    def own(c):
        return pltpu.make_async_copy(
            sent.at[me_h, c], ext[c].at[me_h, pl.ds(row_blocks, row_blocks)], own_in.at[c]
        )

    def halo(piece, c, p, side, mine=False):
        _, device, place = sides[side]
        if mine:
            source = sent.at[me_h, c, of_part(p)]
        else:
            source = ext[c].at[piece, of_part(p, row_blocks)]
        return pltpu.make_async_remote_copy(
            src_ref=source,
            dst_ref=ext[c].at[piece, of_part(p, place * row_blocks)],
            send_sem=halo_send.at[side, piece, c, p],
            recv_sem=halo_recv.at[side, piece, c, p],
            device_id=device,
            device_id_type=MESH,
        )

    def direct_halo(c, p, t, side):
        _, device, s, place = direct[t][side]
        return pltpu.make_async_remote_copy(
            src_ref=sent.at[s, c, of_part(p)],
            dst_ref=ext[c].at[me_h, of_part(p, place * row_blocks)],
            send_sem=direct_send.at[t, c, p],
            recv_sem=halo_recv.at[side, me_h, c, p],
            device_id=device,
            device_id_type=MESH,
        )

    def depart(c, p, side):
        bent = (p, side) in bends
        if bent:
            landing, done = held.at[p, c], bend_recv.at[p, c]
        else:
            landing = ext[c].at[me_h, of_part(p, sides[side][2] * row_blocks)]
            done = halo_recv.at[side, me_h, c, p]
        return pltpu.make_async_remote_copy(
            src_ref=sent.at[group[side], c, of_part(p)],
            dst_ref=landing,
            send_sem=depart_send.at[c, p],
            recv_sem=done,
            device_id=(me_h, way_n(p, side, me_h)) if bent else goal[side],
            device_id_type=MESH,
        )

    def relay_on(c, p, side):
        return pltpu.make_async_remote_copy(
            src_ref=held.at[p, c],
            dst_ref=ext[c].at[me_h, of_part(p, sides[side][2] * row_blocks)],
            send_sem=bend_send.at[p, c],
            recv_sem=halo_recv.at[side, me_h, c, p],
            device_id=goal[side],
            device_id_type=MESH,
        )

    def relay(c):
        for p, side in bends:

            @pl.when(at_way(p, side))
            def _(p=p, side=side):
                depart(c, p, side).wait_recv()
                relay_on(c, p, side).start()

    def piece_of(d):
        return lax.rem(me_h - d + n_harm, n_harm)

    def forwards(d, side):
        piece = piece_of(d)
        if side == 0:
            skip = straight(piece, me_h - 1) | (me_h == mid)
            return has_prev & jnp.logical_not(at_first & skip)
        skip = straight(piece, me_h + 1) | (me_h + 1 == mid)
        return has_next & jnp.logical_not(at_last & skip)

    def start_halo(d, c, p):
        for side in range(2):

            @pl.when(forwards(d, side))
            def _(side=side):
                halo(piece_of(d), c, p, side, mine=d == 0).start()

    order = ORDER if n_harm == 4 else list(range(1, n_harm))
    if DYN and n_harm == 4:
        order = [jnp.int32(2), jnp.where(low, 3, 1), jnp.where(low, 1, 3)]
    back_order = order
    if PREF and n_harm == 4:
        odd = me_h % 2
        back_order = [2 - odd, 3 - odd, 1 + 2 * odd]
        if PREF == 2:
            back_order = [2 - odd, 1 + 2 * odd, 3 - odd]

    def send(c):
        for side in range(2):

            @pl.when(origin[side])
            def _(side=side):
                for p in range(PARTS):
                    depart(c, p, side).start()

        if LAST[c] == 3:
            for p in range(PARTS):
                arrive(order[-1], c, p).start()
        for p in range(PARTS):
            for d in order if LAST[c] < 2 else order[:-1]:
                arrive(d, c, p).start()
        if LAST[c] == 2:
            for p in range(PARTS):
                arrive(order[-1], c, p).start()
        for p in range(PARTS):
            start_halo(0, c, p)
            for t in range(n_harm - 1):
                for side in range(2):

                    @pl.when(direct[t][side][0])
                    def _(t=t, side=side, p=p):
                        direct_halo(c, p, t, side).start()

        own(c).start()

    adj_loads[0].wait()
    spread(0)
    expected = jnp.int32(n_harm - 1)
    for there, _ in greeted:
        expected = expected + jnp.where(there, jnp.int32(1), jnp.int32(0))
    pl.semaphore_wait(barrier, expected)
    send(0)
    for c in range(1, n_chunk):
        adj_loads[c].wait()
        spread(c)
        relay(c - 1)
        send(c)

    half = chunk_rows // 2
    for c in range(n_chunk):
        row = lax.broadcasted_iota(jnp.int32, (chunk_rows, 128), 0)
        k = (row // ROWS) * (n_chunk * ROWS) + c * ROWS + row % ROWS
        half_k = n_harm * n_chunk * ROWS // 2
        rate = jnp.where(k < half_k, k, half_k - k).astype(jnp.float32)
        rate_k[c * chunk_rows : (c + 1) * chunk_rows, :] = rate

    for load in loads:
        load.wait()

    zone_row = lax.broadcasted_iota(jnp.int32, (128, WIDTH), 0)

    def select_step(i, carry):
        at = pl.ds(pl.multiple_of(i * WIDTH, WIDTH), WIDTH)
        hit = zone_row == (zone[:, at] - (pos - 1) * ZONE_DEV)
        w = weight[:, at]
        high = w.astype(jnp.bfloat16).astype(jnp.float32)
        select[0:128, at] = jnp.where(hit, high, 0.0).astype(jnp.bfloat16)
        select[128:256, at] = jnp.where(hit, w - high, 0.0).astype(jnp.bfloat16)
        return carry

    lax.fori_loop(0, nodes // WIDTH, select_step, 0)
    relay(n_chunk - 1)

    def block_of(c, index):
        return jnp.concatenate([ext[c][h, index] for h in range(n_harm)], axis=0)

    def local_part(p):
        def local_step(i, carry):
            at = pl.ds(pl.multiple_of(i * WIDTH, WIDTH), WIDTH)
            first = row_blocks + i * (WIDTH // 128)
            pieces = [
                jnp.concatenate([block_of(c, first + t) for t in range(WIDTH // 128)], axis=1)
                for c in range(n_chunk)
            ]
            field = jnp.concatenate(pieces, axis=0) if n_chunk > 1 else pieces[0]
            samples = jnp.dot(fourier[...], field, preferred_element_type=jnp.float32)
            weighted = (rad[:, at].astype(jnp.float32) * samples).astype(jnp.bfloat16)
            radiative = jnp.dot(fourier_t[...], weighted, preferred_element_type=jnp.float32)
            cap = capacity[:, at]
            for c in range(n_chunk):
                lam = pieces[c].astype(jnp.float32)
                swapped = jnp.concatenate([lam[half:], lam[:half]], axis=0)
                rows = slice(c * chunk_rows, (c + 1) * chunk_rows)
                k = jnp.concatenate([rate_k[rows, :]] * (WIDTH // 128), axis=1)
                rate = k * swapped
                rest = src[:, c, :, at].reshape(chunk_rows, WIDTH) - (cap * rate + radiative[rows])
                src[:, c, :, at] = rest.reshape(n_harm, ROWS, WIDTH)
            return carry

        steps = nodes // PARTS // WIDTH
        lax.fori_loop(p * steps, (p + 1) * steps, local_step, 0)

    def back(d, c, p):
        peer = lax.rem(me_h + d, n_harm)
        return pltpu.make_async_remote_copy(
            src_ref=upd.at[peer, c, of_part(p)],
            dst_ref=ret.at[me_h, c, of_part(p)],
            send_sem=out_send.at[d, c, p],
            recv_sem=out_recv.at[d, c, p],
            device_id=(peer, me_n),
            device_id_type=MESH,
        )

    def own_back(c, p):
        return pltpu.make_async_copy(
            upd.at[me_h, c, of_part(p)], ret.at[me_h, c, of_part(p)], own_out.at[c, p]
        )

    def conduct(c, p):
        def block_step(i, carry):
            b = p * per_part + i
            at = pl.ds(pl.multiple_of(b * 128, 128), 128)
            lam = block_of(c, row_blocks + b)
            taken = [lam]
            for s in range(1, slots):
                col = cols[s, b] - (pos - 1) * row_blocks
                col = jnp.minimum(jnp.maximum(col, 0), 3 * row_blocks - 1)
                taken.append(block_of(c, col))
            conductance = jnp.concatenate([blk[b, s] for s in range(slots)], axis=1)
            conduction = lax.dot_general(
                jnp.concatenate(taken, axis=1),
                conductance,
                NT,
                preferred_element_type=jnp.float32,
            )
            residual = src[:, c, :, at].reshape(chunk_rows, 128) - conduction
            new = lam.astype(jnp.float32) + inv_diag[:, at] * residual
            upd[:, c, b] = new.astype(jnp.bfloat16).reshape(n_harm, ROWS, 128)
            return carry

        lax.fori_loop(0, per_part, block_step, 0, unroll=2)
        if c < n_chunk - 1 or p < PARTS - HOLD:
            give(c, p)

    def give(c, p):
        own_back(c, p).start()
        back(back_order[0], c, p).start()
        if c < n_chunk - 1 or DEFER == 0:
            for d in back_order[1:]:
                back(d, c, p).start()
        else:
            flush = range(p - DEFER, PARTS if p == PARTS - 1 else p - DEFER + 1)
            for late in flush:
                if late >= 0:
                    for d in back_order[1:]:
                        back(d, c, late).start()

    def wait_halo(c):
        for side in range(2):

            @pl.when(sides[1 - side][0])
            def _(side=side):
                for p in range(PARTS):
                    for piece in range(n_harm):
                        halo(piece, c, p, side).wait_recv()

    def take(c, p):
        if p == 0:
            own(c).wait()
        for d in range(1, n_harm):
            arrive(d, c, p).wait_recv()
            start_halo(d, c, p)

    final = n_chunk - 1
    for c in range(final):
        for p in range(PARTS):
            take(c, p)
    done = 0
    for p in range(PARTS):
        take(final, p)
        local_part(p)
        if final > 0 and p >= EARLY:
            if done == 0:
                wait_halo(0)
            while done < p - LAG + 1:
                conduct(0, done)
                done += 1
    for c in range(n_chunk):
        if c > 0 or done == 0:
            wait_halo(c)
        for p in range(done if c == 0 else 0, PARTS):
            conduct(c, p)

    part[...] = jnp.zeros_like(part)
    wide = 512 // 128

    def gradient_step(i, carry):
        at = pl.ds(pl.multiple_of(i * 512, 512), 512)
        new = jnp.concatenate(
            [
                upd[:, :, i * wide + t].reshape(n_harm * n_chunk * ROWS, 128)
                for t in range(wide)
            ],
            axis=1,
        )
        both = lax.dot_general(select[:, at], new, NT, preferred_element_type=jnp.float32)
        part[...] += both[0:128] + both[128:256]
        return carry

    lax.fori_loop(0, nodes // 512, gradient_step, 0)

    def hand_over(side):
        _, device, place = sides[side]
        rows = pl.ds(0 if side == 0 else 2 * ZONE_DEV, ZONE_DEV)
        return pltpu.make_async_remote_copy(
            src_ref=part.at[rows, :],
            dst_ref=from_next if side == 0 else from_prev,
            send_sem=part_send.at[side],
            recv_sem=part_recv.at[side],
            device_id=device,
            device_id_type=MESH,
        )

    for side in range(2):

        @pl.when(sides[side][0])
        def _(side=side):
            hand_over(side).start()

    for p in range(PARTS - HOLD, PARTS):
        give(n_chunk - 1, p)

    grad[...] = part[ZONE_DEV : 2 * ZONE_DEV, :]

    def join():
        for side, buffer in ((0, from_next), (1, from_prev)):

            @pl.when(sides[1 - side][0])
            def _(side=side, buffer=buffer):
                hand_over(side).wait_recv()
                grad[...] += buffer[...]

    def gather(c, p):
        def step(i, carry):
            b = p * per_part + i * TILES
            at = pl.ds(pl.multiple_of(b * 128, 128), TILES * 128)
            for s in range(n_harm):
                for t in range(TILES):
                    stage[pl.ds(t * tile_rows + s, ROWS, stride=n_harm), :] = ret[
                        s, c, b + t
                    ].astype(jnp.float32)
            x = jnp.concatenate(
                [stage[t * tile_rows : (t + 1) * tile_rows, :] for t in range(TILES)], axis=1
            )
            x = x.astype(jnp.bfloat16).reshape(ROWS, n_harm, TILES * 128)
            out[c * ROWS : (c + 1) * ROWS, :, at] = x
            return carry

        lax.fori_loop(0, per_part // TILES, step, 0)

    for c in range(n_chunk):
        for p in range(PARTS):
            own_back(c, p).wait()
            for d in range(1, n_harm):
                back(d, c, p).wait_recv()
            gather(c, p)
            if c == n_chunk - 1 and p == PARTS - 2:
                join()

    for c in range(n_chunk):
        for p in range(PARTS):
            for d in range(1, n_harm):
                arrive(d, c, p).wait_send()
                back(d, c, p).wait_send()
            for side in range(2):
                for t in range(n_harm - 1):

                    @pl.when(direct[t][side][0])
                    def _(t=t, side=side, c=c, p=p):
                        direct_halo(c, p, t, side).wait_send()

                for d in range(n_harm):

                    @pl.when(forwards(d, side))
                    def _(side=side, d=d, c=c, p=p):
                        halo(piece_of(d), c, p, side, mine=d == 0).wait_send()

    for c in range(n_chunk):
        for side in range(2):

            @pl.when(origin[side])
            def _(c=c, side=side):
                for p in range(PARTS):
                    depart(c, p, side).wait_send()

        for p, side in bends:

            @pl.when(at_way(p, side))
            def _(c=c, p=p, side=side):
                relay_on(c, p, side).wait_send()

    for side in range(2):

        @pl.when(sides[side][0])
        def _(side=side):
            hand_over(side).wait_send()


def write_out(updated, gradient, out, grad, sems):
    rows = updated.shape[0] // SLICES
    copies = [pltpu.make_async_copy(gradient, grad, sems.at[SLICES])]
    for i in range(SLICES):
        at = pl.ds(i * rows, rows)
        copies.append(pltpu.make_async_copy(updated.at[at], out.at[at], sems.at[i]))
    for copy in copies:
        copy.start()
    for copy in copies:
        copy.wait()


def body(
    n_harm,
    n_node,
    adjoint,
    source,
    rad_coeff,
    capacity,
    inv_diag,
    blocks,
    block_cols,
    zone_of,
    heater_weight,
):
    rows, _, nodes = adjoint.shape
    n_chunk = rows // ROWS
    harmonics = n_harm * rows
    order = np.arange(harmonics).reshape(n_harm, n_chunk, ROWS).transpose(1, 0, 2).reshape(-1)
    basis = fourier_basis(harmonics)

    row_blocks = nodes // 128
    vmem = pl.BlockSpec(memory_space=pltpu.VMEM)
    hbm = pl.BlockSpec(memory_space=pltpu.HBM)
    piece = (n_harm, n_chunk, ROWS, nodes)
    tiles = (n_harm, n_chunk, row_blocks, ROWS, 128)
    line = (1, nodes)
    dma = pltpu.SemaphoreType.DMA
    updated, gradient = pl.pallas_call(
        functools.partial(kernel, n_harm, n_node, n_chunk),
        out_shape=(
            jax.ShapeDtypeStruct(adjoint.shape, jnp.bfloat16),
            jax.ShapeDtypeStruct((ZONE_DEV, harmonics), jnp.float32),
        ),
        in_specs=[hbm] * 11,
        out_specs=(vmem, vmem),
        scratch_shapes=[pltpu.VMEM((n_harm, 3 * row_blocks, ROWS, 128), jnp.bfloat16)] * n_chunk
        + [
            pltpu.VMEM(adjoint.shape, jnp.bfloat16),
            pltpu.VMEM(piece, jnp.float32),
            pltpu.VMEM(rad_coeff.shape, jnp.bfloat16),
            pltpu.VMEM(blocks.shape, jnp.bfloat16),
            pltpu.VMEM(line, jnp.float32),
            pltpu.VMEM(line, jnp.float32),
            pltpu.VMEM(line, jnp.float32),
            pltpu.VMEM(line, jnp.int32),
            pltpu.SMEM(block_cols.shape[::-1], jnp.int32),
            pltpu.VMEM((harmonics, harmonics), jnp.bfloat16),
            pltpu.VMEM((harmonics, harmonics), jnp.bfloat16),
            pltpu.VMEM((TILES * n_harm * ROWS, 128), jnp.float32),
            pltpu.VMEM(tiles, jnp.bfloat16),
            pltpu.VMEM((harmonics, 128), jnp.float32),
            pltpu.VMEM(tiles, jnp.bfloat16),
            pltpu.VMEM(tiles, jnp.bfloat16),
            pltpu.VMEM((256, nodes), jnp.bfloat16),
            pltpu.VMEM((128, harmonics), jnp.float32),
            pltpu.VMEM((ZONE_DEV, harmonics), jnp.float32),
            pltpu.VMEM((ZONE_DEV, harmonics), jnp.float32),
            dma((10,)),
            dma((n_chunk,)),
            dma((n_chunk,)),
            dma((n_harm, n_chunk, PARTS)),
            dma((n_harm, n_chunk, PARTS)),
            dma((2, n_harm, n_chunk, PARTS)),
            dma((2, n_harm, n_chunk, PARTS)),
            dma((n_harm - 1, n_chunk, PARTS)),
            dma((n_harm, n_chunk, PARTS)),
            dma((n_harm, n_chunk, PARTS)),
            dma((n_chunk, PARTS)),
            dma((2,)),
            dma((2,)),
            pltpu.VMEM((PARTS, n_chunk, row_blocks // PARTS, ROWS, 128), jnp.bfloat16),
            dma((n_chunk, PARTS)),
            dma((PARTS, n_chunk)),
            dma((PARTS, n_chunk)),
        ],
        compiler_params=pltpu.CompilerParams(
            collective_id=0, has_side_effects=True, vmem_limit_bytes=48 * 2**20
        ),
    )(
        *(
            pltpu.with_memory_space_constraint(x, pltpu.HBM)
            for x in (
                adjoint,
                source.reshape(piece),
                rad_coeff,
                blocks,
                capacity[None, :],
                inv_diag[None, :],
                heater_weight[None, :],
                zone_of[None, :],
                block_cols.T,
                jnp.asarray(basis[:, order]),
                jnp.asarray(basis.T[order]),
            )
        )
    )
    return pl.pallas_call(
        write_out,
        out_shape=(
            jax.ShapeDtypeStruct(updated.shape, updated.dtype),
            jax.ShapeDtypeStruct(gradient.shape, gradient.dtype),
        ),
        in_specs=[vmem, vmem],
        out_specs=(hbm, hbm),
        scratch_shapes=[dma((SLICES + 1,))],
    )(
        pltpu.with_memory_space_constraint(updated, pltpu.VMEM),
        pltpu.with_memory_space_constraint(gradient, pltpu.VMEM),
    )


def solution(mesh):
    in_specs = (
        P("harm", None, "node"),
        P(None, ("harm", "node")),
        P(None, ("harm", "node")),
        P(("harm", "node")),
        P(("harm", "node")),
        P(("harm", "node"), None, None, None),
        P(("harm", "node"), None),
        P(("harm", "node")),
        P(("harm", "node")),
    )
    out_specs = (P("harm", None, "node"), P(("harm", "node"), None))
    step = functools.partial(body, mesh.shape["harm"], mesh.shape["node"])
    return jax.shard_map(step, mesh=mesh, in_specs=in_specs, out_specs=out_specs, check_vma=False)
```
